256 devices in a mesh: seq: 32 (over x, z), kvh: 8 (over y, core).
Axes of the slice: x: 4, y: 4, z: 8, core: 2. Of those that a mesh axis runs over, the one named last changes fastest.
Arguments:
- queries: bfloat16 [512, 8192], P('seq', 'kvh'), may hold values from -240 to 240
- trace_cache_keys: bfloat16 [131072, 1024], P('seq', 'kvh'), may hold values from -7 to 7
- trace_cache_values: bfloat16 [131072, 1024], P('seq', 'kvh'), may hold values from -6 to 6
- out_weight: bfloat16 [8192, 8192], P('kvh', 'seq'), may hold values from -0.0625 to 0.0625
- positions: int32 [512], P('seq'), may hold values from 1 to 131072, as said below
- partner: int32 [512], replicated, may hold values from 0 to 511, as said below
Outputs:
- mixed: bfloat16 [512, 8192], P('kvh', 'seq')
- contrast: bfloat16 [512, 8192], P('kvh', 'seq')
The draws below stay inside these ranges and needn't reach their ends.
Inputs may be any that keep to these rules, and one draw needn't show every extreme that they name: Token t sees trace positions 0 to positions[t] - 1; some token sees all 131072 positions. partner pairs the tokens: partner[partner[t]] = t and partner[t] != t.
All inputs are finite; a program needn't handle non-finite values.
Results may differ from the reference program's by a relative error of at most 0.01.
Values may be sent and summed in bfloat16 or wider, within the bound.
A program may use at most 64 MiB of HBM per device.

```python
import math
import jax
import jax.numpy as jnp
from jax import lax

D = 8192
QUERY_HEADS = 64
KEY_VALUE_HEADS = 8
HEAD_SIZE = 128
CACHE_PER_SHARD = 4096
TOKEN_COUNT = 512
CACHE_POSITIONS = 131072
N_SEQ = 32


def trace_layout(key):
    key = jax.random.fold_in(key, 7)
    first = jax.random.fold_in(key, 0)
    second = jax.random.fold_in(key, 1)
    fourth_part = jax.random.fold_in(key, 3)
    positions = jax.random.randint(first, (TOKEN_COUNT,), 1, CACHE_POSITIONS + 1)
    farthest = jax.random.randint(second, (), 0, TOKEN_COUNT)
    positions = positions.at[farthest].set(CACHE_POSITIONS)
    drawn_base_keys = jnp.clip(jax.random.normal(fourth_part, (CACHE_POSITIONS, KEY_VALUE_HEADS * HEAD_SIZE), jnp.float32), -6.0, 6.0)
    return (positions, drawn_base_keys)


def draw_positions(key, part):
    return trace_layout(key)[0]


def draw_trace_cache_keys(key, part):
    positions, drawn_base_keys = trace_layout(key)
    return drawn_base_keys.astype(jnp.bfloat16)


def draw_queries(key, part):
    key = jax.random.fold_in(key, 2)
    field = 3.0 * jnp.clip(jax.random.normal(key, (TOKEN_COUNT, QUERY_HEADS * HEAD_SIZE), jnp.float32), -6.0, 6.0)
    return field.astype(jnp.bfloat16)


def draw_partner(key, part):
    key = jax.random.fold_in(key, 3)
    order = jax.random.permutation(key, TOKEN_COUNT)
    chosen_branch = order[0::2]
    rejected = order[1::2]
    partner = jnp.zeros((TOKEN_COUNT,), jnp.int32)
    partner = partner.at[chosen_branch].set(rejected)
    partner = partner.at[rejected].set(chosen_branch)
    return partner


def level_of(own_key, extent, pieces, low, largest):
    level = 1.0
    for position, shards_of in pieces:
        draws = jax.random.uniform(jax.random.fold_in(jax.random.fold_in(own_key, 6), position), (shards_of,), jnp.float32, low / len(pieces), largest / len(pieces))
        level = level * jnp.repeat(jnp.exp(draws), extent[position] // shards_of).reshape((-1,) + (1,) * (len(extent) - 1 - position))
    return level


def centred(own_key, shape, width, bound, pieces=(), kind=jnp.bfloat16):
    result = jax.random.normal(own_key, shape, jnp.float32) * width
    if len(pieces) > 0:
        result = level_of(own_key, shape, pieces, -0.22, 0.18) * result
    return jnp.clip(result, min=-bound, max=bound).astype(kind)


def setup_inputs(seed: int = 0) -> dict:
    seeds = jax.random.split(jax.random.key(seed), 7)
    queries = draw_queries(jax.random.fold_in(seeds[6], 71), 0)
    trace_cache_keys = draw_trace_cache_keys(jax.random.fold_in(seeds[6], 71), 0)
    trace_cache_values = centred(seeds[2], (CACHE_POSITIONS, KEY_VALUE_HEADS * HEAD_SIZE), 1.0, 6.0, ((0, 32), (1, 8)))
    out_weight = centred(seeds[3], (QUERY_HEADS * HEAD_SIZE, D), (QUERY_HEADS * HEAD_SIZE) ** -0.5, 0.0625, ((0, 8), (1, 32)))
    positions = draw_positions(jax.random.fold_in(seeds[6], 71), 0)
    partner = draw_partner(jax.random.fold_in(seeds[6], 71), 0)
    return dict(queries=queries, trace_cache_keys=trace_cache_keys, trace_cache_values=trace_cache_values, out_weight=out_weight, positions=positions, partner=partner)


lowest = -1e+30

def head_terms(query_head, key_head, value_head, positions, start):
    scores = jnp.einsum('tgd,cd->tgc', query_head, key_head.astype(jnp.float32)) * (1.0 / math.sqrt(HEAD_SIZE))
    token_count = key_head.shape[0]
    seen = (start + lax.iota(jnp.int32, token_count))[None, :] < positions[:, None]
    seen = seen[:, None, :]
    block_max = lax.optimization_barrier(jnp.max(jnp.where(seen, scores, lowest), axis=-1))
    weights = jnp.where(seen, jnp.exp(scores - block_max[..., None]), 0.0)
    block_total = lax.optimization_barrier(jnp.sum(weights, axis=-1))
    weights16 = weights.astype(jnp.bfloat16)
    block_out = jnp.einsum('tgc,cd->tgd', weights16.astype(jnp.float32), value_head.astype(jnp.float32))
    return (block_max, block_total, block_out)

def reference(queries, trace_cache_keys, trace_cache_values, out_weight, positions, partner):
    query_group = QUERY_HEADS // KEY_VALUE_HEADS
    grouped_queries = queries.astype(jnp.float32).reshape(TOKEN_COUNT, KEY_VALUE_HEADS, query_group, HEAD_SIZE).transpose(1, 0, 2, 3)
    key_block_list = trace_cache_keys.reshape(N_SEQ, CACHE_PER_SHARD, KEY_VALUE_HEADS, HEAD_SIZE).transpose(0, 2, 1, 3)
    value_block_list = trace_cache_values.reshape(N_SEQ, CACHE_PER_SHARD, KEY_VALUE_HEADS, HEAD_SIZE).transpose(0, 2, 1, 3)

    def block(inputs):
        key_blk, value_blk, index = inputs
        start = (index * CACHE_PER_SHARD).astype(jnp.int32)

        def head(head_inputs):
            return head_terms(head_inputs[0], head_inputs[1], head_inputs[2], positions, start)
        return lax.map(head, (grouped_queries, key_blk, value_blk))
    block_max, block_total, block_out = lax.map(block, (key_block_list, value_block_list, jnp.arange(N_SEQ, dtype=jnp.int32)))
    top = lax.optimization_barrier(jnp.max(block_max, axis=0))
    factor = jnp.exp(block_max - top)
    numerator = lax.optimization_barrier(jnp.sum(factor[..., None] * block_out, axis=0))
    denominator = lax.optimization_barrier(jnp.sum(factor * block_total, axis=0))
    attended = (numerator / denominator[..., None]).transpose(1, 0, 2, 3).reshape(TOKEN_COUNT, QUERY_HEADS * HEAD_SIZE).astype(jnp.bfloat16)
    mixed = jnp.dot(attended, out_weight, preferred_element_type=jnp.float32).astype(jnp.bfloat16)
    other = jnp.take(mixed, partner, axis=0)
    contrast = (mixed.astype(jnp.float32) - other.astype(jnp.float32)).astype(jnp.bfloat16)
    return (mixed, contrast)
```

```python
import math

import jax
import jax.numpy as jnp
from jax import lax
from jax.experimental import pallas as pl
from jax.experimental.pallas import tpu as pltpu
from jax.sharding import PartitionSpec as P

MESH = pl.DeviceIdType.MESH

HEADS = 8
HEAD = 128
NX, NZ, NK = 4, 8, 8
LENGTH = 4096
TOK = 16
CHUNK = NZ * TOK
TOKENS = NX * CHUNK
COLS = HEADS * HEAD
WIDE = COLS + 128
OUT = 256
SHARE = TOKENS // NK

GROUP = 4
ROWS = GROUP * CHUNK
STEP = 1024

LOW = -1e30
SCALE2 = math.log2(math.e) / math.sqrt(HEAD)


def dot(a, b):
    return lax.dot_general(a, b, (((1,), (0,)), ((), ())), preferred_element_type=jnp.float32)


def spread(t):
    lane = lax.broadcasted_iota(jnp.int32, t.shape, 1)
    t = jnp.where(lane < 8, t, 0.0)
    t = t + pltpu.roll(t, 8, 1) + pltpu.roll(t, 16, 1)
    first = t.astype(jnp.bfloat16).astype(jnp.float32)
    rest = t - first
    second = rest.astype(jnp.bfloat16).astype(jnp.float32)
    third = rest - second
    return jnp.where(lane < 8, first, jnp.where(lane < 16, second, third)).astype(jnp.bfloat16)


def gathered(t):
    t = t.astype(jnp.float32)
    return t + pltpu.roll(t, 120, 1) + pltpu.roll(t, 112, 1)


def merge(tiles, outs):
    logs = [gathered(t) for t in tiles]
    top = logs[0]
    for u in logs[1:]:
        top = jnp.maximum(top, u)
    shares = [jnp.exp2(u - top) for u in logs]
    total = shares[0]
    for w in shares[1:]:
        total = total + w
    inverse = 1.0 / total
    shares = [w * inverse for w in shares]
    merged = []
    for h in range(HEADS):
        acc = None
        for w, o in zip(shares, outs):
            term = w[:, h : h + 1] * o(h).astype(jnp.float32)
            acc = term if acc is None else acc + term
        merged.append(acc.astype(jnp.bfloat16))
    return merged, top + jnp.log2(total)


def kernel(
    q_ref, k_ref, v_ref, w_ref, pos_ref, partner_ref, mixed_ref, contrast_ref,
    k_buf, v_buf, w_buf, kt, vp, s0, s1, run, q_all, part, part_in, lse, zpart, z_in, att, pairs, terms, t_in,
    local_sem, qz_send, qz_recv, qx_send, qx_recv, px_send, px_recv, pz_send, pz_recv,
    az_send, az_recv, ax_send, ax_recv, t_send, t_recv,
):
    seq = lax.axis_index("seq")
    kvh = lax.axis_index("kvh")
    x = seq // NZ
    z = seq % NZ

    def x_peer(d):
        return (((x + d) % NX) * NZ + z, kvh)

    def z_peer(d):
        return (x * NZ + (z + d) % NZ, kvh)

    def k_peer(d):
        return (seq, (kvh + d) % NK)

    def block(i):
        return pl.ds(pl.multiple_of(i * TOK, TOK), TOK)

    loads = [
        pltpu.make_async_copy(src, dst, local_sem.at[i])
        for i, (src, dst) in enumerate(((k_ref, k_buf), (v_ref, v_buf), (w_ref, w_buf)))
    ]
    for c in loads:
        c.start()

    barrier = pltpu.get_barrier_semaphore()
    for d in range(1, NX):
        pl.semaphore_signal(barrier, inc=1, device_id=x_peer(d), device_id_type=MESH)
    for d in range(1, NZ):
        pl.semaphore_signal(barrier, inc=1, device_id=z_peer(d), device_id_type=MESH)
    for d in range(1, NK):
        pl.semaphore_signal(barrier, inc=1, device_id=k_peer(d), device_id_type=MESH)

    row = lax.broadcasted_iota(jnp.int32, (TOK, 128), 0)
    lane = lax.broadcasted_iota(jnp.int32, (TOK, 128), 1)
    counts = jnp.zeros((TOK, 128), jnp.int32)
    for i in range(TOK):
        counts = jnp.where(row == i, pos_ref[i], counts)
    high = lax.shift_right_logical(counts, 12)
    middle = lax.bitwise_and(lax.shift_right_logical(counts, 4), 255)
    low = lax.bitwise_and(counts, 15)
    counts = jnp.where(lane == 0, high, jnp.where(lane == 1, middle, low))
    q_all[x, block(z), 0:COLS] = q_ref[...]
    q_all[x, block(z), COLS:WIDE] = counts.astype(jnp.float32).astype(jnp.bfloat16)

    pl.semaphore_wait(barrier, NX + NZ + NK - 3)

    def qz(d):
        return pltpu.make_async_remote_copy(
            src_ref=q_all.at[x, block(z)], dst_ref=q_all.at[x, block(z)],
            send_sem=qz_send.at[d - 1], recv_sem=qz_recv.at[d - 1], device_id=z_peer(d), device_id_type=MESH)

    def qx(d):
        return pltpu.make_async_remote_copy(
            src_ref=q_all.at[x], dst_ref=q_all.at[x],
            send_sem=qx_send.at[d - 1], recv_sem=qx_recv.at[d - 1], device_id=x_peer(d), device_id_type=MESH)

    def px(d, half):
        owner = (x + d) % NX
        cols = pl.ds(0, 512) if half == 0 else pl.ds(512, WIDE - 512)
        return pltpu.make_async_remote_copy(
            src_ref=part.at[owner, :, cols], dst_ref=part_in.at[d - 1, :, cols],
            send_sem=px_send.at[half, d - 1], recv_sem=px_recv.at[half, d - 1], device_id=x_peer(d), device_id_type=MESH)

    def pz(d):
        return pltpu.make_async_remote_copy(
            src_ref=zpart.at[block((z + d) % NZ)], dst_ref=z_in.at[d - 1],
            send_sem=pz_send.at[d - 1], recv_sem=pz_recv.at[d - 1], device_id=z_peer(d), device_id_type=MESH)

    def az(d):
        return pltpu.make_async_remote_copy(
            src_ref=att.at[x, block(z)], dst_ref=att.at[x, block(z)],
            send_sem=az_send.at[d - 1], recv_sem=az_recv.at[d - 1], device_id=z_peer(d), device_id_type=MESH)

    def ax(d):
        return pltpu.make_async_remote_copy(
            src_ref=att.at[x], dst_ref=att.at[x],
            send_sem=ax_send.at[d - 1], recv_sem=ax_recv.at[d - 1], device_id=x_peer(d), device_id_type=MESH)

    def tk(d):
        rows = pl.ds(pl.multiple_of(((kvh + d) % NK) * SHARE, SHARE), SHARE)
        return pltpu.make_async_remote_copy(
            src_ref=terms.at[rows], dst_ref=t_in.at[kvh],
            send_sem=t_send.at[d - 1], recv_sem=t_recv.at[d - 1], device_id=k_peer(d), device_id_type=MESH)

    for d in range(1, NZ):
        qz(d).start()

    loads[0].wait()
    kt[...] = k_buf[...].T
    loads[1].wait()
    vp[:, 0:HEAD] = v_buf[...]
    vp[:, HEAD:] = jnp.where(lax.broadcasted_iota(jnp.int32, (LENGTH, 128), 1) == 0, 1.0, 0.0).astype(jnp.bfloat16)
    pairs[...] = jnp.where(
        lax.broadcasted_iota(jnp.int32, (TOKENS, TOKENS), 0) == partner_ref[...], 1.0, 0.0).astype(jnp.bfloat16)
    loads[2].wait()

    for d in range(1, NZ):
        qz(d).wait_recv()
    for d in range(1, NX):
        qx(d).start()

    start = seq * LENGTH
    run_of = (run.at[0], run.at[1])

    def offset(p):
        return p + p // 2 - 2 * (p // 3)

    def attention(a_chunk, a_half, b_chunk, b_half):
        if a_chunk is not None:
            a_x = (x + offset(a_chunk)) % NX
            q = jnp.concatenate(
                [q_all[a_x, :, (a_half * GROUP + j) * HEAD : (a_half * GROUP + j + 1) * HEAD] for j in range(GROUP)], axis=0)
            c = q_all[a_x, :, COLS:WIDE].astype(jnp.float32)
            count = (c[:, 0:1] * 4096.0 + c[:, 1:2] * 16.0 + c[:, 2:3]).astype(jnp.int32) - start
            a_s = (s0, s1)[a_half]
            a_run = None
        if b_chunk is not None:
            b_s = (s0, s1)[b_half]
            top = jnp.maximum(jnp.max(run_of[b_half][...], axis=1, keepdims=True), -1e29)
            total = None
        for i in range(LENGTH // STEP):
            cols = pl.ds(i * STEP, STEP)
            if a_chunk is not None:
                s = dot(q, kt[:, cols]) * SCALE2
                seen = (i * STEP + lax.broadcasted_iota(jnp.int32, (CHUNK, STEP), 1)) < count
                s = jnp.where(seen[None], s.reshape(GROUP, CHUNK, STEP), LOW).reshape(ROWS, STEP)
                a_s[:, cols] = s
                for j in range(STEP // 128):
                    m = s[:, j * 128 : (j + 1) * 128]
                    a_run = m if a_run is None else jnp.maximum(a_run, m)
            if b_chunk is not None:
                o = dot(jnp.exp2(b_s[:, cols] - top).astype(jnp.bfloat16), vp[cols, :])
                total = o if total is None else total + o
        if a_chunk is not None:
            run_of[a_half][...] = a_run
        if b_chunk is not None:
            b_x = (x + offset(b_chunk)) % NX
            weight = total[:, HEAD : HEAD + 1]
            some = weight > 0.0
            weight = jnp.where(some, weight, 1.0)
            out = total[:, 0:HEAD] / weight
            log = jnp.where(some, top + jnp.log2(weight), LOW)
            lanes = lax.broadcasted_iota(jnp.int32, (CHUNK, 128), 1)
            tile = jnp.zeros((CHUNK, 128), jnp.float32) if b_half == 0 else lse[...]
            for j in range(GROUP):
                h = b_half * GROUP + j
                part[b_x, :, h * HEAD : (h + 1) * HEAD] = out[j * CHUNK : (j + 1) * CHUNK].astype(jnp.bfloat16)
                tile = jnp.where(lanes == h, log[j * CHUNK : (j + 1) * CHUNK], tile)
            if b_half == 0:
                lse[...] = tile
            else:
                part[b_x, :, COLS:WIDE] = spread(tile)

    attention(0, 0, None, None)

    def pair(p, _):
        attention(p, 1, p, 0)

        @pl.when(p > 0)
        def _():
            px(offset(p), 0).start()

        qx(NX - offset(p + 1)).wait_recv()
        attention(p + 1, 0, p, 1)

        @pl.when(p > 0)
        def _():
            px(offset(p), 1).start()

        return 0

    lax.fori_loop(0, NX - 1, pair, 0)
    attention(NX - 1, 1, NX - 1, 0)
    px(2, 0).start()
    attention(None, None, NX - 1, 1)
    px(2, 1).start()

    for d in (1, 3, 2):
        px(d, 0).wait_recv()
        px(d, 1).wait_recv()
    own = lambda h: part[x, :, h * HEAD : (h + 1) * HEAD]
    others = [lambda h, d=d: part_in[d, :, h * HEAD : (h + 1) * HEAD] for d in range(NX - 1)]
    merged, log = merge([part[x, :, COLS:WIDE]] + [part_in[d, :, COLS:WIDE] for d in range(NX - 1)], [own] + others)
    for h in range(HEADS):
        zpart[:, h * HEAD : (h + 1) * HEAD] = merged[h]
    zpart[:, COLS:WIDE] = spread(log)
    for d in range(1, NZ):
        pz(d).start()

    for d in range(1, NZ):
        pz(d).wait_recv()
    own = lambda h: zpart[block(z), h * HEAD : (h + 1) * HEAD]
    others = [lambda h, d=d: z_in[d, :, h * HEAD : (h + 1) * HEAD] for d in range(NZ - 1)]
    merged, _ = merge([zpart[block(z), COLS:WIDE]] + [z_in[d, :, COLS:WIDE] for d in range(NZ - 1)], [own] + others)
    for h in range(HEADS):
        att[x, block(z), h * HEAD : (h + 1) * HEAD] = merged[h]

    for d in range(1, NZ):
        az(d).start()
    for d in range(1, NZ):
        az(d).wait_recv()
    for d in range(1, NX):
        ax(d).start()

    def project(source):
        rows = pl.ds(pl.multiple_of(source * CHUNK, CHUNK), CHUNK)
        terms[rows, 0:OUT] = dot(att[source], w_buf[...]).astype(jnp.bfloat16)

    project(x)
    for d in (1, 3, 2):
        ax(d).wait_recv()
        project((x + NX - d) % NX)

    terms[:, OUT:] = dot(pairs[...], terms[:, 0:OUT]).astype(jnp.bfloat16)
    for d in range(1, NK):
        tk(d).start()
    t_in[kvh] = terms[pl.ds(pl.multiple_of(kvh * SHARE, SHARE), SHARE)]
    for d in range(1, NK):
        tk(d).wait_recv()
    total = t_in[0].astype(jnp.float32)
    for i in range(1, NK):
        total = total + t_in[i].astype(jnp.float32)
    total = total.astype(jnp.bfloat16)
    mixed_ref[...] = total[:, 0:OUT]
    contrast_ref[...] = (total[:, 0:OUT].astype(jnp.float32) - total[:, OUT:].astype(jnp.float32)).astype(jnp.bfloat16)

    for d in range(1, NX):
        qx(d).wait_send()
        px(d, 0).wait_send()
        px(d, 1).wait_send()
        ax(d).wait_send()
    for d in range(1, NZ):
        qz(d).wait_send()
        pz(d).wait_send()
        az(d).wait_send()
    for d in range(1, NK):
        tk(d).wait_send()


def per_device(queries, keys, values, out_weight, positions, partner):
    bf, f32 = jnp.bfloat16, jnp.float32
    vmem = pl.BlockSpec(memory_space=pltpu.VMEM)
    any_ = pl.BlockSpec(memory_space=pl.ANY)
    dma = pltpu.SemaphoreType.DMA
    return pl.pallas_call(
        kernel,
        out_shape=(jax.ShapeDtypeStruct((SHARE, OUT), bf),) * 2,
        in_specs=[vmem, any_, any_, any_, pl.BlockSpec(memory_space=pltpu.SMEM), vmem],
        out_specs=(vmem, vmem),
        scratch_shapes=[
            pltpu.VMEM((LENGTH, HEAD), bf),
            pltpu.VMEM((LENGTH, HEAD), bf),
            pltpu.VMEM((COLS, OUT), bf),
            pltpu.VMEM((HEAD, LENGTH), bf),
            pltpu.VMEM((LENGTH, 2 * HEAD), bf),
            pltpu.VMEM((ROWS, LENGTH), f32),
            pltpu.VMEM((ROWS, LENGTH), f32),
            pltpu.VMEM((2, ROWS, 128), f32),
            pltpu.VMEM((NX, CHUNK, WIDE), bf),
            pltpu.VMEM((NX, CHUNK, WIDE), bf),
            pltpu.VMEM((NX - 1, CHUNK, WIDE), bf),
            pltpu.VMEM((CHUNK, 128), f32),
            pltpu.VMEM((CHUNK, WIDE), bf),
            pltpu.VMEM((NZ - 1, TOK, WIDE), bf),
            pltpu.VMEM((NX, CHUNK, COLS), bf),
            pltpu.VMEM((TOKENS, TOKENS), bf),
            pltpu.VMEM((TOKENS, 2 * OUT), bf),
            pltpu.VMEM((NK, SHARE, 2 * OUT), bf),
            dma((3,)),
            dma((NZ - 1,)), dma((NZ - 1,)),
            dma((NX - 1,)), dma((NX - 1,)),
            dma((2, NX - 1)), dma((2, NX - 1)),
            dma((NZ - 1,)), dma((NZ - 1,)),
            dma((NZ - 1,)), dma((NZ - 1,)),
            dma((NX - 1,)), dma((NX - 1,)),
            dma((NK - 1,)), dma((NK - 1,)),
        ],
        compiler_params=pltpu.CompilerParams(
            collective_id=0, has_side_effects=True, vmem_limit_bytes=56 * 2**20),
    )(queries, keys, values, out_weight, positions, partner.reshape(1, TOKENS))


def solution(mesh):
    placed = (P("seq", "kvh"), P("seq", "kvh"), P("seq", "kvh"), P("kvh", "seq"), P("seq"), P())
    return jax.shard_map(
        per_device,
        mesh=mesh,
        in_specs=placed,
        out_specs=(P("kvh", "seq"), P("kvh", "seq")),
        check_vma=False,
    )
```

```python
import math

import jax
import jax.numpy as jnp
from jax import lax
from jax.experimental import pallas as pl
from jax.experimental.pallas import tpu as pltpu
from jax.sharding import PartitionSpec as P

MESH = pl.DeviceIdType.MESH

HEADS = 8
HEAD = 128
NX, NZ, NK = 4, 8, 8
LENGTH = 4096
TOK = 16
CHUNK = NZ * TOK
TOKENS = NX * CHUNK
COLS = HEADS * HEAD
WIDE = COLS + 128
OUT = 256
SHARE = TOKENS // NK

SLAB = NX * TOK
ROWS = HEADS * SLAB
STEP = 1024

LOW = -1e30
SCALE2 = math.log2(math.e) / math.sqrt(HEAD)


def dot(a, b):
    return lax.dot_general(a, b, (((1,), (0,)), ((), ())), preferred_element_type=jnp.float32)


def spread(t):
    lane = lax.broadcasted_iota(jnp.int32, t.shape, 1)
    t = jnp.where(lane < 8, t, 0.0)
    t = t + pltpu.roll(t, 8, 1) + pltpu.roll(t, 16, 1)
    first = t.astype(jnp.bfloat16).astype(jnp.float32)
    rest = t - first
    second = rest.astype(jnp.bfloat16).astype(jnp.float32)
    third = rest - second
    return jnp.where(lane < 8, first, jnp.where(lane < 16, second, third)).astype(jnp.bfloat16)


def gathered(t):
    t = t.astype(jnp.float32)
    return t + pltpu.roll(t, 120, 1) + pltpu.roll(t, 112, 1)


def merge(tiles, outs):
    logs = [gathered(t) for t in tiles]
    top = logs[0]
    for u in logs[1:]:
        top = jnp.maximum(top, u)
    shares = [jnp.exp2(u - top) for u in logs]
    total = shares[0]
    for w in shares[1:]:
        total = total + w
    inverse = 1.0 / total
    shares = [w * inverse for w in shares]
    merged = []
    for h in range(HEADS):
        acc = None
        for w, o in zip(shares, outs):
            term = w[:, h : h + 1] * o(h).astype(jnp.float32)
            acc = term if acc is None else acc + term
        merged.append(acc.astype(jnp.bfloat16))
    return merged, top + jnp.log2(total)


def kernel(
    q_ref, k_ref, v_ref, w_ref, pos_ref, partner_ref, total_ref,
    k_buf, v_buf, w_buf, kt, vp, s0, s1, run, q_all, part, part_in, zpart, z_in, att, pairs, terms, t_out, t_in, p_out, p_in,
    local_sem, qx_send, qx_recv, up_send, up_recv, down_send, down_recv, px_send, px_recv, pz_send, pz_recv,
    az_send, az_recv, right_send, right_recv, left_send, left_recv, far_send, far_recv, t_send, t_recv, p_send, p_recv,
):
    seq = lax.axis_index("seq")
    kvh = lax.axis_index("kvh")
    x = seq // NZ
    z = seq % NZ

    def x_peer(d):
        return (((x + d) % NX) * NZ + z, kvh)

    def z_peer(d):
        return (x * NZ + (z + d) % NZ, kvh)

    def k_peer(d):
        return (seq, (kvh + d) % NK)

    def block(i):
        return pl.ds(pl.multiple_of(i * TOK, TOK), TOK)

    def remote(src, dst, send, recv, peer):
        return pltpu.make_async_remote_copy(
            src_ref=src, dst_ref=dst, send_sem=send, recv_sem=recv, device_id=peer, device_id_type=MESH)

    loads = [
        pltpu.make_async_copy(src, dst, local_sem.at[i])
        for i, (src, dst) in enumerate(((k_ref, k_buf), (v_ref, v_buf), (w_ref, w_buf)))
    ]
    for c in loads:
        c.start()

    barrier = pltpu.get_barrier_semaphore()
    for d in range(1, NX):
        pl.semaphore_signal(barrier, inc=1, device_id=x_peer(d), device_id_type=MESH)
    for d in range(1, NZ):
        pl.semaphore_signal(barrier, inc=1, device_id=z_peer(d), device_id_type=MESH)
    for d in range(1, NK):
        pl.semaphore_signal(barrier, inc=1, device_id=k_peer(d), device_id_type=MESH)

    row = lax.broadcasted_iota(jnp.int32, (TOK, 128), 0)
    lane = lax.broadcasted_iota(jnp.int32, (TOK, 128), 1)
    counts = jnp.zeros((TOK, 128), jnp.int32)
    for i in range(TOK):
        counts = jnp.where(row == i, pos_ref[i], counts)
    high = lax.shift_right_logical(counts, 12)
    middle = lax.bitwise_and(lax.shift_right_logical(counts, 4), 255)
    low = lax.bitwise_and(counts, 15)
    counts = jnp.where(lane == 0, high, jnp.where(lane == 1, middle, low))
    q_all[z, block(x), 0:COLS] = q_ref[...]
    q_all[z, block(x), COLS:WIDE] = counts.astype(jnp.float32).astype(jnp.bfloat16)

    pl.semaphore_wait(barrier, NX + NZ + NK - 3)

    def qx(d):
        here = q_all.at[z, block(x)]
        return remote(here, here, qx_send.at[d - 1], qx_recv.at[d - 1], x_peer(d))

    def up(k, last=False):
        slab = q_all.at[(z + NZ + 1 - k) % NZ]
        if last:
            slab = slab.at[pl.ds(0, SLAB // 2)]
        return remote(slab, slab, up_send.at[k - 1], up_recv.at[k - 1], z_peer(1))

    def down(k, last=False):
        slab = q_all.at[(z + k - 1) % NZ]
        if last:
            slab = slab.at[pl.ds(SLAB // 2, SLAB // 2)]
        return remote(slab, slab, down_send.at[k - 1], down_recv.at[k - 1], z_peer(NZ - 1))

    def px(n, d):
        return remote(part.at[n, block((x + d) % NX)], part_in.at[n, d - 1],
                      px_send.at[n, d - 1], px_recv.at[n, d - 1], x_peer(d))

    def offset(n):
        m = n + (n // 6) * (13 - 2 * n)
        return ((m + 1) // 2 * (2 * (m % 2) - 1) + NZ) % NZ

    def pz(n):
        return remote(zpart.at[n], z_in.at[n], pz_send.at[n - 1], pz_recv.at[n - 1], z_peer(offset(n)))

    def az(d):
        here = att.at[x, block(z)]
        return remote(here, here, az_send.at[d - 1], az_recv.at[d - 1], z_peer(d))

    def right(d):
        here = att.at[x, block((z + NZ - d) % NZ)]
        return remote(here, here, right_send.at[d], right_recv.at[d], x_peer(1))

    def left(d):
        here = att.at[x, block((z + NZ - d) % NZ)]
        return remote(here, here, left_send.at[d], left_recv.at[d], x_peer(NX - 1))

    def far(d):
        if d % 2 == 0:
            here = att.at[(x + NX - 1) % NX, block((z + NZ - d) % NZ)]
            return remote(here, here, far_send.at[d], far_recv.at[d], x_peer(1))
        here = att.at[(x + 1) % NX, block((z + NZ - d) % NZ)]
        return remote(here, here, far_send.at[d], far_recv.at[d], x_peer(NX - 1))

    def tk(d):
        return remote(t_out.at[(kvh + d) % NK], t_in.at[kvh], t_send.at[d - 1], t_recv.at[d - 1], k_peer(d))

    def pk(d):
        return remote(p_out.at[(kvh + d) % NK], p_in.at[kvh], p_send.at[d - 1], p_recv.at[d - 1], k_peer(d))

    for d in range(1, NX):
        qx(d).start()

    loads[0].wait()
    kt[...] = k_buf[...].T

    for d in range(1, NX):
        qx(d).wait_recv()
    up(1).start()
    down(1).start()

    start = seq * LENGTH
    run_of = (run.at[0], run.at[1])

    def attention(a, a_slot, b, b_slot):
        if a is not None:
            a_z = (z + offset(a)) % NZ
            q = jnp.concatenate([q_all[a_z, :, h * HEAD : (h + 1) * HEAD] for h in range(HEADS)], axis=0)
            c = q_all[a_z, :, COLS:WIDE].astype(jnp.float32)
            count = (c[:, 0:1] * 4096.0 + c[:, 1:2] * 16.0 + c[:, 2:3]).astype(jnp.int32) - start
            a_s = (s0, s1)[a_slot]
            a_run = None
        if b is not None:
            b_s = (s0, s1)[b_slot]
            top = jnp.maximum(jnp.max(run_of[b_slot][...], axis=1, keepdims=True), -1e29)
            total = None
        for i in range(LENGTH // STEP):
            cols = pl.ds(i * STEP, STEP)
            if a is not None:
                s = dot(q, kt[:, cols]) * SCALE2
                seen = (i * STEP + lax.broadcasted_iota(jnp.int32, (SLAB, STEP), 1)) < count
                s = jnp.where(seen[None], s.reshape(HEADS, SLAB, STEP), LOW).reshape(ROWS, STEP)
                a_s[:, cols] = s
                for j in range(STEP // 128):
                    m = s[:, j * 128 : (j + 1) * 128]
                    a_run = m if a_run is None else jnp.maximum(a_run, m)
            if b is not None:
                o = dot(jnp.exp2(b_s[:, cols] - top).astype(jnp.bfloat16), vp[cols, :])
                total = o if total is None else total + o
        if a is not None:
            run_of[a_slot][...] = a_run
        if b is not None:
            weight = total[:, HEAD : HEAD + 1]
            some = weight > 0.0
            weight = jnp.where(some, weight, 1.0)
            out = total[:, 0:HEAD] / weight
            log = jnp.where(some, top + jnp.log2(weight), LOW)
            lanes = lax.broadcasted_iota(jnp.int32, (SLAB, 128), 1)
            tile = jnp.zeros((SLAB, 128), jnp.float32)
            for h in range(HEADS):
                part[b, :, h * HEAD : (h + 1) * HEAD] = out[h * SLAB : (h + 1) * SLAB].astype(jnp.bfloat16)
                tile = jnp.where(lanes == h, log[h * SLAB : (h + 1) * SLAB], tile)
            part[b, :, COLS:WIDE] = spread(tile)
            for d in range(1, NX):
                px(b, d).start()

    def over_x(n):
        for d in range(1, NX):
            px(n, d).wait_recv()
        outs = [lambda h: part[n, block(x), h * HEAD : (h + 1) * HEAD]]
        outs += [lambda h, d=d: part_in[n, d, :, h * HEAD : (h + 1) * HEAD] for d in range(NX - 1)]
        tiles = [part[n, block(x), COLS:WIDE]] + [part_in[n, d, :, COLS:WIDE] for d in range(NX - 1)]
        merged, log = merge(tiles, outs)
        for h in range(HEADS):
            zpart[n, :, h * HEAD : (h + 1) * HEAD] = merged[h]
        zpart[n, :, COLS:WIDE] = spread(log)

    attention(0, 0, None, None)
    loads[1].wait()
    vp[:, 0:HEAD] = v_buf[...]
    vp[:, HEAD:] = jnp.where(lax.broadcasted_iota(jnp.int32, (LENGTH, 128), 1) == 0, 1.0, 0.0).astype(jnp.bfloat16)
    pairs[...] = jnp.where(
        lax.broadcasted_iota(jnp.int32, (TOKENS, TOKENS), 0) == partner_ref[...], 1.0, 0.0).astype(jnp.bfloat16)
    loads[2].wait()

    def two(j, _):
        up(j + 1).wait_recv()
        down(j + 1).wait_recv()

        @pl.when(j < 2)
        def _():
            up(j + 2).start()
            down(j + 2).start()

        @pl.when(j == 2)
        def _():
            up(4, True).start()
            down(4, True).start()

        attention(2 * j + 1, 1, 2 * j, 0)

        @pl.when(j > 0)
        def _():
            over_x(2 * j - 1)
            pz(2 * j - 1).start()

        @pl.when(j == 2)
        def _():
            up(4, True).wait_recv()
            down(4, True).wait_recv()

        attention(2 * j + 2, 0, 2 * j + 1, 1)
        over_x(2 * j)

        @pl.when(j > 0)
        def _():
            pz(2 * j).start()

        return 0

    lax.fori_loop(0, NZ // 2 - 1, two, 0)
    attention(NZ - 1, 1, NZ - 2, 0)
    over_x(NZ - 3)
    pz(NZ - 3).start()
    attention(None, None, NZ - 1, 1)
    over_x(NZ - 2)
    pz(NZ - 2).start()
    over_x(NZ - 1)
    pz(NZ - 1).start()

    for n in range(1, NZ):
        pz(n).wait_recv()
    outs = [lambda h: zpart[0, :, h * HEAD : (h + 1) * HEAD]]
    outs += [lambda h, n=n: z_in[n, :, h * HEAD : (h + 1) * HEAD] for n in range(1, NZ)]
    merged, _ = merge([zpart[0, :, COLS:WIDE]] + [z_in[n, :, COLS:WIDE] for n in range(1, NZ)], outs)
    for h in range(HEADS):
        att[x, block(z), h * HEAD : (h + 1) * HEAD] = merged[h]

    order = (0, 1, 7, 2, 6, 3, 5, 4)
    for d in order[1:]:
        az(d).start()

    def relay(d):
        (right if d % 2 == 0 else left)(d).wait_recv()
        far(d).start()

    for i, d in enumerate(order):
        if d > 0:
            az(d).wait_recv()
        right(d).start()
        left(d).start()
        if i >= 2:
            relay(order[i - 2])

    def project(source):
        rows = pl.ds(pl.multiple_of(source * CHUNK, CHUNK), CHUNK)
        t = dot(att[source], w_buf[...]).astype(jnp.bfloat16)
        terms[rows] = t
        for j in range(CHUNK // SHARE):
            owner = source * (CHUNK // SHARE) + j
            t_out[owner] = t[j * SHARE : (j + 1) * SHARE]

            @pl.when(owner != kvh)
            def _():
                tk((owner + NK - kvh) % NK).start()

    project(x)
    relay(order[6])
    relay(order[7])
    for d in order:
        (left if d % 2 == 0 else right)(d).wait_recv()
    project((x + 1) % NX)
    project((x + NX - 1) % NX)
    for d in order:
        far(d).wait_recv()
    project((x + 2) % NX)

    partners = dot(pairs[...], terms[...]).astype(jnp.bfloat16)
    for i in range(NK):
        p_out[i] = partners[i * SHARE : (i + 1) * SHARE]
    for d in range(1, NK):
        pk(d).start()
    t_in[kvh] = t_out[kvh]
    p_in[kvh] = p_out[kvh]

    def total(ref):
        t = ref[0].astype(jnp.float32)
        for i in range(1, NK):
            t = t + ref[i].astype(jnp.float32)
        return t.astype(jnp.bfloat16)

    for d in range(1, NK):
        tk(d).wait_recv()
    total_ref[:, 0:OUT] = total(t_in)
    for d in range(1, NK):
        pk(d).wait_recv()
    total_ref[:, OUT:] = total(p_in)

    for d in range(1, NX):
        qx(d).wait_send()
        for n in range(NZ):
            px(n, d).wait_send()
    for k in range(1, NZ // 2 + 1):
        up(k, k == NZ // 2).wait_send()
        down(k, k == NZ // 2).wait_send()
    for d in range(1, NZ):
        pz(d).wait_send()
        az(d).wait_send()
    for d in range(NZ):
        right(d).wait_send()
        left(d).wait_send()
        far(d).wait_send()
    for d in range(1, NK):
        tk(d).wait_send()
        pk(d).wait_send()


def per_device(queries, keys, values, out_weight, positions, partner):
    bf, f32 = jnp.bfloat16, jnp.float32
    vmem = pl.BlockSpec(memory_space=pltpu.VMEM)
    any_ = pl.BlockSpec(memory_space=pl.ANY)
    dma = pltpu.SemaphoreType.DMA
    total = pl.pallas_call(
        kernel,
        out_shape=jax.ShapeDtypeStruct((SHARE, 2 * OUT), bf),
        in_specs=[vmem, any_, any_, any_, pl.BlockSpec(memory_space=pltpu.SMEM), vmem],
        out_specs=vmem,
        scratch_shapes=[
            pltpu.VMEM((LENGTH, HEAD), bf),
            pltpu.VMEM((LENGTH, HEAD), bf),
            pltpu.VMEM((COLS, OUT), bf),
            pltpu.VMEM((HEAD, LENGTH), bf),
            pltpu.VMEM((LENGTH, 2 * HEAD), bf),
            pltpu.VMEM((ROWS, LENGTH), f32),
            pltpu.VMEM((ROWS, LENGTH), f32),
            pltpu.VMEM((2, ROWS, 128), f32),
            pltpu.VMEM((NZ, SLAB, WIDE), bf),
            pltpu.VMEM((NZ, SLAB, WIDE), bf),
            pltpu.VMEM((NZ, NX - 1, TOK, WIDE), bf),
            pltpu.VMEM((NZ, TOK, WIDE), bf),
            pltpu.VMEM((NZ, TOK, WIDE), bf),
            pltpu.VMEM((NX, CHUNK, COLS), bf),
            pltpu.VMEM((TOKENS, TOKENS), bf),
            pltpu.VMEM((TOKENS, OUT), bf),
            pltpu.VMEM((NK, SHARE, OUT), bf),
            pltpu.VMEM((NK, SHARE, OUT), bf),
            pltpu.VMEM((NK, SHARE, OUT), bf),
            pltpu.VMEM((NK, SHARE, OUT), bf),
            dma((3,)),
            dma((NX - 1,)), dma((NX - 1,)),
            dma((4,)), dma((4,)), dma((4,)), dma((4,)),
            dma((NZ, NX - 1)), dma((NZ, NX - 1)),
            dma((NZ - 1,)), dma((NZ - 1,)),
            dma((NZ - 1,)), dma((NZ - 1,)),
            dma((NZ,)), dma((NZ,)), dma((NZ,)), dma((NZ,)), dma((NZ,)), dma((NZ,)),
            dma((NK - 1,)), dma((NK - 1,)), dma((NK - 1,)), dma((NK - 1,)),
        ],
        compiler_params=pltpu.CompilerParams(
            collective_id=0, has_side_effects=True, vmem_limit_bytes=56 * 2**20),
    )(queries, keys, values, out_weight, positions, partner.reshape(1, TOKENS))
    mixed, other = total[:, 0:OUT], total[:, OUT:]
    return mixed, (mixed.astype(f32) - other.astype(f32)).astype(bf)


def solution(mesh):
    placed = (P("seq", "kvh"), P("seq", "kvh"), P("seq", "kvh"), P("kvh", "seq"), P("seq"), P())
    return jax.shard_map(
        per_device,
        mesh=mesh,
        in_specs=placed,
        out_specs=(P("kvh", "seq"), P("kvh", "seq")),
        check_vma=False,
    )
```

```python
import math

import jax
import jax.numpy as jnp
from jax import lax
from jax.experimental import pallas as pl
from jax.experimental.pallas import tpu as pltpu
from jax.sharding import PartitionSpec as P

MESH = pl.DeviceIdType.MESH

HEADS = 8
HEAD = 128
NX, NZ, NK = 4, 8, 8
LENGTH = 4096
TOK = 16
CHUNK = NZ * TOK
TOKENS = NX * CHUNK
COLS = HEADS * HEAD
WIDE = COLS + 128
OUT = 256
SHARE = TOKENS // NK

SLAB = NX * TOK
ROWS = HEADS * SLAB
STEP = 1024

LOW = -1e30
SCALE2 = math.log2(math.e) / math.sqrt(HEAD)


def dot(a, b):
    return lax.dot_general(a, b, (((1,), (0,)), ((), ())), preferred_element_type=jnp.float32)


def dot_t(a, b):
    return lax.dot_general(a, b, (((1,), (1,)), ((), ())), preferred_element_type=jnp.float32)


def spread(t):
    lane = lax.broadcasted_iota(jnp.int32, t.shape, 1)
    t = jnp.where(lane < 8, t, 0.0)
    t = t + pltpu.roll(t, 8, 1) + pltpu.roll(t, 16, 1)
    first = t.astype(jnp.bfloat16).astype(jnp.float32)
    rest = t - first
    second = rest.astype(jnp.bfloat16).astype(jnp.float32)
    third = rest - second
    return jnp.where(lane < 8, first, jnp.where(lane < 16, second, third)).astype(jnp.bfloat16)


def gathered(t):
    t = t.astype(jnp.float32)
    return t + pltpu.roll(t, 120, 1) + pltpu.roll(t, 112, 1)


def merge(tiles, outs):
    logs = [gathered(t) for t in tiles]
    top = logs[0]
    for u in logs[1:]:
        top = jnp.maximum(top, u)
    shares = [jnp.exp2(u - top) for u in logs]
    total = shares[0]
    for w in shares[1:]:
        total = total + w
    inverse = 1.0 / total
    shares = [w * inverse for w in shares]
    merged = []
    for h in range(HEADS):
        acc = None
        for w, o in zip(shares, outs):
            term = w[:, h : h + 1] * o(h).astype(jnp.float32)
            acc = term if acc is None else acc + term
        merged.append(acc.astype(jnp.bfloat16))
    return merged, top + jnp.log2(total)


def kernel(
    q_ref, k_ref, v_ref, w_ref, pos_ref, partner_ref, total_ref,
    k_buf, v_buf, w_buf, vp, s0, s1, run, q_all, part, part_in, zpart, z_in, att, pairs, terms, t_out, t_in, p_out, p_in,
    local_sem, fq_send, fq_recv, up_send, up_recv, down_send, down_recv, px_send, px_recv, pz_send, pz_recv,
    az_send, az_recv, ax_send, ax_recv, t_send, t_recv, p_send, p_recv,
):
    seq = lax.axis_index("seq")
    kvh = lax.axis_index("kvh")
    x = seq // NZ
    z = seq % NZ

    def x_peer(d):
        return (((x + d) % NX) * NZ + z, kvh)

    def z_peer(d):
        return (x * NZ + (z + d) % NZ, kvh)

    def k_peer(d):
        return (seq, (kvh + d) % NK)

    def block(i):
        return pl.ds(pl.multiple_of(i * TOK, TOK), TOK)

    def remote(src, dst, send, recv, peer):
        return pltpu.make_async_remote_copy(
            src_ref=src, dst_ref=dst, send_sem=send, recv_sem=recv, device_id=peer, device_id_type=MESH)

    loads = [
        pltpu.make_async_copy(src, dst, local_sem.at[i])
        for i, (src, dst) in enumerate(((k_ref, k_buf), (v_ref, v_buf), (w_ref, w_buf)))
    ]
    for c in loads:
        c.start()

    barrier = pltpu.get_barrier_semaphore()
    for d in range(1, NX):
        pl.semaphore_signal(barrier, inc=1, device_id=x_peer(d), device_id_type=MESH)
    for d in (1, NZ - 1):
        pl.semaphore_signal(barrier, inc=1, device_id=z_peer(d), device_id_type=MESH)
    for d in range(1, NK):
        pl.semaphore_signal(barrier, inc=1, device_id=k_peer(d), device_id_type=MESH)

    row = lax.broadcasted_iota(jnp.int32, (TOK, 128), 0)
    lane = lax.broadcasted_iota(jnp.int32, (TOK, 128), 1)
    counts = jnp.zeros((TOK, 128), jnp.int32)
    for i in range(TOK):
        counts = jnp.where(row == i, pos_ref[i], counts)
    high = lax.shift_right_logical(counts, 12)
    middle = lax.bitwise_and(lax.shift_right_logical(counts, 4), 255)
    low = lax.bitwise_and(counts, 15)
    counts = jnp.where(lane == 0, high, jnp.where(lane == 1, middle, low))
    q_all[z, block(x), 0:COLS] = q_ref[...]
    q_all[z, block(x), COLS:WIDE] = counts.astype(jnp.float32).astype(jnp.bfloat16)

    pl.semaphore_wait(barrier, NX + NK)

    def up(k):
        here = q_all.at[(z + NZ + 1 - k) % NZ, block(x)]
        return remote(here, here, up_send.at[k - 1], up_recv.at[k - 1], z_peer(1))

    def down(k):
        here = q_all.at[(z + k - 1) % NZ, block(x)]
        return remote(here, here, down_send.at[k - 1], down_recv.at[k - 1], z_peer(NZ - 1))

    def fq(dz, e):
        here = q_all.at[(z + dz) % NZ, block(x)]
        return remote(here, here, fq_send.at[dz, e - 1], fq_recv.at[dz, e - 1], x_peer(e))

    def hop(k):
        up(k).wait_recv()
        if k < NZ // 2:
            down(k).wait_recv()
            up(k + 1).start()
        if k + 1 < NZ // 2:
            down(k + 1).start()
        for e in (1, 3, 2):
            fq(NZ - k, e).start()
            if k < NZ // 2:
                fq(k, e).start()

    def px(n, d):
        return remote(part.at[n, block((x + d) % NX)], part_in.at[n, d - 1],
                      px_send.at[n, d - 1], px_recv.at[n, d - 1], x_peer(d))

    order = (0, 1, 7, 2, 6, 3, 4, 5)

    def pz(n):
        return remote(zpart.at[n], z_in.at[n], pz_send.at[n - 1], pz_recv.at[n - 1], z_peer(order[n]))

    def az(d):
        here = att.at[x, block(z)]
        return remote(here, here, az_send.at[d - 1], az_recv.at[d - 1], z_peer(d))

    def ax(d, e):
        here = att.at[x, block((z + NZ - d) % NZ)]
        return remote(here, here, ax_send.at[d, e - 1], ax_recv.at[d, e - 1], x_peer(e))

    def tk(d):
        return remote(t_out.at[(kvh + d) % NK], t_in.at[kvh], t_send.at[d - 1], t_recv.at[d - 1], k_peer(d))

    def pk(d):
        return remote(p_out.at[(kvh + d) % NK], p_in.at[kvh], p_send.at[d - 1], p_recv.at[d - 1], k_peer(d))

    up(1).start()
    down(1).start()
    for e in (1, 3, 2):
        fq(0, e).start()

    loads[1].wait()
    vp[:, 0:HEAD] = v_buf[...]
    vp[:, HEAD:] = jnp.where(lax.broadcasted_iota(jnp.int32, (LENGTH, 128), 1) == 0, 1.0, 0.0).astype(jnp.bfloat16)
    loads[0].wait()

    start = seq * LENGTH
    run_of = (run.at[0], run.at[1])

    def attention(a, a_slot, b, b_slot, done=None):
        if done is not None:
            for d in range(1, NX):
                px(done, d).wait_recv()
        if a is not None:
            for e in (1, 3, 2):
                fq(order[a], e).wait_recv()
            if a == 0:
                hop(1)
            a_z = (z + order[a]) % NZ
            q = jnp.concatenate([q_all[a_z, :, h * HEAD : (h + 1) * HEAD] for h in range(HEADS)], axis=0)
            c = q_all[a_z, :, COLS:WIDE].astype(jnp.float32)
            count = (c[:, 0:1] * 4096.0 + c[:, 1:2] * 16.0 + c[:, 2:3]).astype(jnp.int32) - start
            a_s = (s0, s1)[a_slot]
            a_run = None
        if b is not None:
            b_s = (s0, s1)[b_slot]
            top = jnp.maximum(jnp.max(run_of[b_slot][...], axis=1, keepdims=True), -1e29)
            total = None
        for i in range(LENGTH // STEP):
            cols = pl.ds(i * STEP, STEP)
            if a is not None:
                s = dot_t(q, k_buf[cols, :]) * SCALE2
                seen = (i * STEP + lax.broadcasted_iota(jnp.int32, (SLAB, STEP), 1)) < count
                s = jnp.where(seen[None], s.reshape(HEADS, SLAB, STEP), LOW).reshape(ROWS, STEP)
                a_s[:, cols] = s
                for j in range(STEP // 128):
                    m = s[:, j * 128 : (j + 1) * 128]
                    a_run = m if a_run is None else jnp.maximum(a_run, m)
            if b is not None:
                o = dot(jnp.exp2(b_s[:, cols] - top).astype(jnp.bfloat16), vp[cols, :])
                total = o if total is None else total + o
            if done is not None and i == 1:
                over_x(done)
        if a is not None:
            run_of[a_slot][...] = a_run
        if b is not None:
            weight = total[:, HEAD : HEAD + 1]
            some = weight > 0.0
            weight = jnp.where(some, weight, 1.0)
            out = total[:, 0:HEAD] / weight
            log = jnp.where(some, top + jnp.log2(weight), LOW)
            lanes = lax.broadcasted_iota(jnp.int32, (SLAB, 128), 1)
            tile = jnp.zeros((SLAB, 128), jnp.float32)
            for h in range(HEADS):
                part[b, :, h * HEAD : (h + 1) * HEAD] = out[h * SLAB : (h + 1) * SLAB].astype(jnp.bfloat16)
                tile = jnp.where(lanes == h, log[h * SLAB : (h + 1) * SLAB], tile)
            part[b, :, COLS:WIDE] = spread(tile)
            for d in range(1, NX):
                px(b, d).start()
        if done is not None and done > 0:
            pz(done).start()

    def over_x(n):
        outs = [lambda h: part[n, block(x), h * HEAD : (h + 1) * HEAD]]
        outs += [lambda h, d=d: part_in[n, d, :, h * HEAD : (h + 1) * HEAD] for d in range(NX - 1)]
        tiles = [part[n, block(x), COLS:WIDE]] + [part_in[n, d, :, COLS:WIDE] for d in range(NX - 1)]
        merged, log = merge(tiles, outs)
        for h in range(HEADS):
            zpart[n, :, h * HEAD : (h + 1) * HEAD] = merged[h]
        zpart[n, :, COLS:WIDE] = spread(log)

    attention(0, 0, None, None)
    pairs[...] = jnp.where(
        lax.broadcasted_iota(jnp.int32, (TOKENS, TOKENS), 0) == partner_ref[...], 1.0, 0.0).astype(jnp.bfloat16)
    attention(None, None, 0, 0)
    loads[2].wait()

    hop(2)
    attention(1, 1, None, None)
    attention(2, 0, 1, 1)
    hop(3)
    attention(3, 1, 2, 0, 0)
    hop(4)
    attention(4, 0, 3, 1, 1)
    attention(5, 1, 4, 0, 2)
    attention(6, 0, 5, 1, 3)
    attention(7, 1, 6, 0, 4)
    attention(None, None, 7, 1, 5)
    for n in (NZ - 2, NZ - 1):
        for d in range(1, NX):
            px(n, d).wait_recv()
        over_x(n)
        pz(n).start()

    for n in range(1, NZ):
        pz(n).wait_recv()
    outs = [lambda h: zpart[0, :, h * HEAD : (h + 1) * HEAD]]
    outs += [lambda h, n=n: z_in[n, :, h * HEAD : (h + 1) * HEAD] for n in range(1, NZ)]
    merged, _ = merge([zpart[0, :, COLS:WIDE]] + [z_in[n, :, COLS:WIDE] for n in range(1, NZ)], outs)
    for h in range(HEADS):
        att[x, block(z), h * HEAD : (h + 1) * HEAD] = merged[h]

    near = (0, 1, 7, 2, 6, 3, 5, 4)
    for e in (1, 3, 2):
        ax(0, e).start()
    for d in near[1:]:
        az(d).start()
    for d in near[1:]:
        az(d).wait_recv()
        for e in (1, 3, 2):
            ax(d, e).start()

    def project(source):
        rows = pl.ds(pl.multiple_of(source * CHUNK, CHUNK), CHUNK)
        t = dot(att[source], w_buf[...]).astype(jnp.bfloat16)
        terms[rows] = t
        for j in range(CHUNK // SHARE):
            owner = source * (CHUNK // SHARE) + j
            t_out[owner] = t[j * SHARE : (j + 1) * SHARE]

            @pl.when(owner != kvh)
            def _():
                tk((owner + NK - kvh) % NK).start()

    project(x)
    for e in (1, 3, 2):
        for d in near:
            ax(d, e).wait_recv()
        project((x + NX - e) % NX)

    partners = dot(pairs[...], terms[...]).astype(jnp.bfloat16)
    for i in range(NK):
        p_out[i] = partners[i * SHARE : (i + 1) * SHARE]
    for d in range(1, NK):
        pk(d).start()
    t_in[kvh] = t_out[kvh]
    p_in[kvh] = p_out[kvh]

    def total(ref):
        t = ref[0].astype(jnp.float32)
        for i in range(1, NK):
            t = t + ref[i].astype(jnp.float32)
        return t.astype(jnp.bfloat16)

    for d in range(1, NK):
        tk(d).wait_recv()
    total_ref[:, 0:OUT] = total(t_in)
    for d in range(1, NK):
        pk(d).wait_recv()
    total_ref[:, OUT:] = total(p_in)

    for n in range(NZ):
        for e in range(1, NX):
            fq(n, e).wait_send()
            px(n, e).wait_send()
            ax(n, e).wait_send()
    for k in range(1, NZ // 2 + 1):
        up(k).wait_send()
        if k < NZ // 2:
            down(k).wait_send()
    for d in range(1, NZ):
        pz(d).wait_send()
        az(d).wait_send()
    for d in range(1, NK):
        tk(d).wait_send()
        pk(d).wait_send()


def per_device(queries, keys, values, out_weight, positions, partner):
    bf, f32 = jnp.bfloat16, jnp.float32
    vmem = pl.BlockSpec(memory_space=pltpu.VMEM)
    any_ = pl.BlockSpec(memory_space=pl.ANY)
    dma = pltpu.SemaphoreType.DMA
    total = pl.pallas_call(
        kernel,
        out_shape=jax.ShapeDtypeStruct((SHARE, 2 * OUT), bf),
        in_specs=[vmem, any_, any_, any_, pl.BlockSpec(memory_space=pltpu.SMEM), vmem],
        out_specs=vmem,
        scratch_shapes=[
            pltpu.VMEM((LENGTH, HEAD), bf),
            pltpu.VMEM((LENGTH, HEAD), bf),
            pltpu.VMEM((COLS, OUT), bf),
            pltpu.VMEM((LENGTH, 2 * HEAD), bf),
            pltpu.VMEM((ROWS, LENGTH), f32),
            pltpu.VMEM((ROWS, LENGTH), f32),
            pltpu.VMEM((2, ROWS, 128), f32),
            pltpu.VMEM((NZ, SLAB, WIDE), bf),
            pltpu.VMEM((NZ, SLAB, WIDE), bf),
            pltpu.VMEM((NZ, NX - 1, TOK, WIDE), bf),
            pltpu.VMEM((NZ, TOK, WIDE), bf),
            pltpu.VMEM((NZ, TOK, WIDE), bf),
            pltpu.VMEM((NX, CHUNK, COLS), bf),
            pltpu.VMEM((TOKENS, TOKENS), bf),
            pltpu.VMEM((TOKENS, OUT), bf),
            pltpu.VMEM((NK, SHARE, OUT), bf),
            pltpu.VMEM((NK, SHARE, OUT), bf),
            pltpu.VMEM((NK, SHARE, OUT), bf),
            pltpu.VMEM((NK, SHARE, OUT), bf),
            dma((3,)),
            dma((NZ, NX - 1)), dma((NZ, NX - 1)),
            dma((4,)), dma((4,)), dma((4,)), dma((4,)),
            dma((NZ, NX - 1)), dma((NZ, NX - 1)),
            dma((NZ - 1,)), dma((NZ - 1,)),
            dma((NZ - 1,)), dma((NZ - 1,)),
            dma((NZ, NX - 1)), dma((NZ, NX - 1)),
            dma((NK - 1,)), dma((NK - 1,)), dma((NK - 1,)), dma((NK - 1,)),
        ],
        compiler_params=pltpu.CompilerParams(
            collective_id=0, has_side_effects=True, vmem_limit_bytes=56 * 2**20),
    )(queries, keys, values, out_weight, positions, partner.reshape(1, TOKENS))
    mixed, other = total[:, 0:OUT], total[:, OUT:]
    return mixed, (mixed.astype(f32) - other.astype(f32)).astype(bf)


def solution(mesh):
    placed = (P("seq", "kvh"), P("seq", "kvh"), P("seq", "kvh"), P("kvh", "seq"), P("seq"), P())
    return jax.shard_map(
        per_device,
        mesh=mesh,
        in_specs=placed,
        out_specs=(P("kvh", "seq"), P("kvh", "seq")),
        check_vma=False,
    )
```

```python
import math

import jax
import jax.numpy as jnp
from jax import lax
from jax.experimental import pallas as pl
from jax.experimental.pallas import tpu as pltpu
from jax.sharding import PartitionSpec as P

MESH = pl.DeviceIdType.MESH

HEADS = 8
HEAD = 128
NX, NZ, NK = 4, 8, 8
LENGTH = 4096
TOK = 16
CHUNK = NZ * TOK
TOKENS = NX * CHUNK
COLS = HEADS * HEAD
WIDE = COLS + 128
OUT = 256
SHARE = TOKENS // NK

SLAB = NX * TOK
ROWS = HEADS * SLAB
STEP = 1024

LOW = -1e30
SCALE2 = math.log2(math.e) / math.sqrt(HEAD)


def dot(a, b):
    return lax.dot_general(a, b, (((1,), (0,)), ((), ())), preferred_element_type=jnp.float32)


def dot_t(a, b):
    return lax.dot_general(a, b, (((1,), (1,)), ((), ())), preferred_element_type=jnp.float32)


def spread(t):
    lane = lax.broadcasted_iota(jnp.int32, t.shape, 1)
    t = jnp.where(lane < 8, t, 0.0)
    t = t + pltpu.roll(t, 8, 1) + pltpu.roll(t, 16, 1)
    first = t.astype(jnp.bfloat16).astype(jnp.float32)
    rest = t - first
    second = rest.astype(jnp.bfloat16).astype(jnp.float32)
    third = rest - second
    return jnp.where(lane < 8, first, jnp.where(lane < 16, second, third)).astype(jnp.bfloat16)


def gathered(t):
    t = t.astype(jnp.float32)
    return t + pltpu.roll(t, 120, 1) + pltpu.roll(t, 112, 1)


def merge(tiles, outs):
    logs = [gathered(t) for t in tiles]
    top = logs[0]
    for u in logs[1:]:
        top = jnp.maximum(top, u)
    shares = [jnp.exp2(u - top) for u in logs]
    total = shares[0]
    for w in shares[1:]:
        total = total + w
    inverse = 1.0 / total
    shares = [w * inverse for w in shares]
    merged = []
    for h in range(HEADS):
        acc = None
        for w, o in zip(shares, outs):
            term = w[:, h : h + 1] * o(h).astype(jnp.float32)
            acc = term if acc is None else acc + term
        merged.append(acc.astype(jnp.bfloat16))
    return merged, top + jnp.log2(total)


def kernel(
    q_ref, k_ref, v_ref, w_ref, pos_ref, partner_ref, total_ref,
    k_buf, v_buf, w_buf, vp, s0, s1, run, q_all, part, part_in, zpart, z_in, att, pairs, terms, t_out, t_in, p_out, p_in,
    local_sem, fq_send, fq_recv, up_send, up_recv, down_send, down_recv, px_send, px_recv, pz_send, pz_recv,
    az_send, az_recv, ax_send, ax_recv, t_send, t_recv, p_send, p_recv,
):
    seq = lax.axis_index("seq")
    kvh = lax.axis_index("kvh")
    x = seq // NZ
    z = seq % NZ

    def x_peer(d):
        return (((x + d) % NX) * NZ + z, kvh)

    def z_peer(d):
        return (x * NZ + (z + d) % NZ, kvh)

    def k_peer(d):
        return (seq, (kvh + d) % NK)

    def block(i):
        return pl.ds(pl.multiple_of(i * TOK, TOK), TOK)

    def remote(src, dst, send, recv, peer):
        return pltpu.make_async_remote_copy(
            src_ref=src, dst_ref=dst, send_sem=send, recv_sem=recv, device_id=peer, device_id_type=MESH)

    loads = [
        pltpu.make_async_copy(src, dst, local_sem.at[i])
        for i, (src, dst) in enumerate(((k_ref, k_buf), (v_ref, v_buf), (w_ref, w_buf)))
    ]
    for c in loads:
        c.start()

    barrier = pltpu.get_barrier_semaphore()
    for d in range(1, NX):
        pl.semaphore_signal(barrier, inc=1, device_id=x_peer(d), device_id_type=MESH)
    for d in (1, NZ - 1):
        pl.semaphore_signal(barrier, inc=1, device_id=z_peer(d), device_id_type=MESH)
    for d in range(1, NK):
        pl.semaphore_signal(barrier, inc=1, device_id=k_peer(d), device_id_type=MESH)

    row = lax.broadcasted_iota(jnp.int32, (TOK, 128), 0)
    lane = lax.broadcasted_iota(jnp.int32, (TOK, 128), 1)
    counts = jnp.zeros((TOK, 128), jnp.int32)
    for i in range(TOK):
        counts = jnp.where(row == i, pos_ref[i], counts)
    high = lax.shift_right_logical(counts, 12)
    middle = lax.bitwise_and(lax.shift_right_logical(counts, 4), 255)
    low = lax.bitwise_and(counts, 15)
    counts = jnp.where(lane == 0, high, jnp.where(lane == 1, middle, low))
    q_all[z, block(x), 0:COLS] = q_ref[...]
    q_all[z, block(x), COLS:WIDE] = counts.astype(jnp.float32).astype(jnp.bfloat16)

    pl.semaphore_wait(barrier, NX + NK)

    def up(k):
        here = q_all.at[(z + NZ + 1 - k) % NZ, block(x)]
        return remote(here, here, up_send.at[k - 1], up_recv.at[k - 1], z_peer(1))

    def down(k):
        here = q_all.at[(z + k - 1) % NZ, block(x)]
        return remote(here, here, down_send.at[k - 1], down_recv.at[k - 1], z_peer(NZ - 1))

    def fq(dz, e):
        here = q_all.at[(z + dz) % NZ, block(x)]
        return remote(here, here, fq_send.at[dz, e - 1], fq_recv.at[dz, e - 1], x_peer(e))

    def hop(k):
        up(k).wait_recv()
        if k < NZ // 2:
            down(k).wait_recv()
            up(k + 1).start()
        if k + 1 < NZ // 2:
            down(k + 1).start()
        for e in (1, 3, 2):
            fq(NZ - k, e).start()
            if k < NZ // 2:
                fq(k, e).start()

    def px(n, d):
        return remote(part.at[n, block((x + d) % NX)], part_in.at[n, d - 1],
                      px_send.at[n, d - 1], px_recv.at[n, d - 1], x_peer(d))

    order = (0, 1, 7, 2, 6, 3, 4, 5)

    def pz(n):
        return remote(zpart.at[n], z_in.at[n], pz_send.at[n - 1], pz_recv.at[n - 1], z_peer(order[n]))

    def az(d):
        here = att.at[x, block(z)]
        return remote(here, here, az_send.at[d - 1], az_recv.at[d - 1], z_peer(d))

    def ax(d, e):
        here = att.at[x, block((z + NZ - d) % NZ)]
        return remote(here, here, ax_send.at[d, e - 1], ax_recv.at[d, e - 1], x_peer(e))

    def tk(d):
        return remote(t_out.at[(kvh + d) % NK], t_in.at[kvh], t_send.at[d - 1], t_recv.at[d - 1], k_peer(d))

    def pk(d):
        return remote(p_out.at[(kvh + d) % NK], p_in.at[kvh], p_send.at[d - 1], p_recv.at[d - 1], k_peer(d))

    up(1).start()
    down(1).start()
    for e in (1, 3, 2):
        fq(0, e).start()

    loads[1].wait()
    vp[:, 0:HEAD] = v_buf[...]
    vp[:, HEAD:] = jnp.where(lax.broadcasted_iota(jnp.int32, (LENGTH, 128), 1) == 0, 1.0, 0.0).astype(jnp.bfloat16)
    loads[0].wait()

    start = seq * LENGTH
    run_of = (run.at[0], run.at[1])

    def attention(a, dz, a_slot, b, b_slot, done=None):
        if a is not None:
            for e in (1, 3, 2):
                fq(dz, e).wait_recv()
            a_z = (z + dz) % NZ
            q = jnp.concatenate([q_all[a_z, :, h * HEAD : (h + 1) * HEAD] for h in range(HEADS)], axis=0)
            c = q_all[a_z, :, COLS:WIDE].astype(jnp.float32)
            count = (c[:, 0:1] * 4096.0 + c[:, 1:2] * 16.0 + c[:, 2:3]).astype(jnp.int32) - start
            a_s = (s0, s1)[a_slot]
            a_run = None
        if b is not None:
            b_s = (s0, s1)[b_slot]
            top = jnp.maximum(jnp.max(run_of[b_slot][...], axis=1, keepdims=True), -1e29)
            total = None
        for i in range(LENGTH // STEP):
            cols = pl.ds(i * STEP, STEP)
            if a is not None:
                s = dot_t(q, k_buf[cols, :]) * SCALE2
                seen = (i * STEP + lax.broadcasted_iota(jnp.int32, (SLAB, STEP), 1)) < count
                s = jnp.where(seen[None], s.reshape(HEADS, SLAB, STEP), LOW).reshape(ROWS, STEP)
                a_s[:, cols] = s
                for j in range(STEP // 128):
                    m = s[:, j * 128 : (j + 1) * 128]
                    a_run = m if a_run is None else jnp.maximum(a_run, m)
            if b is not None:
                o = dot(jnp.exp2(b_s[:, cols] - top).astype(jnp.bfloat16), vp[cols, :])
                total = o if total is None else total + o
            if done is not None and i == 1:
                over_x(done)
        if a is not None:
            run_of[a_slot][...] = a_run
        if b is not None:
            weight = total[:, HEAD : HEAD + 1]
            some = weight > 0.0
            weight = jnp.where(some, weight, 1.0)
            out = total[:, 0:HEAD] / weight
            log = jnp.where(some, top + jnp.log2(weight), LOW)
            lanes = lax.broadcasted_iota(jnp.int32, (SLAB, 128), 1)
            tile = jnp.zeros((SLAB, 128), jnp.float32)
            for h in range(HEADS):
                part[b, :, h * HEAD : (h + 1) * HEAD] = out[h * SLAB : (h + 1) * SLAB].astype(jnp.bfloat16)
                tile = jnp.where(lanes == h, log[h * SLAB : (h + 1) * SLAB], tile)
            part[b, :, COLS:WIDE] = spread(tile)
            for d in range(1, NX):
                px(b, d).start()

    def over_x(n):
        outs = [lambda h: part[n, block(x), h * HEAD : (h + 1) * HEAD]]
        outs += [lambda h, d=d: part_in[n, d, :, h * HEAD : (h + 1) * HEAD] for d in range(NX - 1)]
        tiles = [part[n, block(x), COLS:WIDE]] + [part_in[n, d, :, COLS:WIDE] for d in range(NX - 1)]
        merged, log = merge(tiles, outs)
        for h in range(HEADS):
            zpart[n, :, h * HEAD : (h + 1) * HEAD] = merged[h]
        zpart[n, :, COLS:WIDE] = spread(log)

    hop(1)
    attention(0, 0, 0, None, None)
    pairs[...] = jnp.where(
        lax.broadcasted_iota(jnp.int32, (TOKENS, TOKENS), 0) == partner_ref[...], 1.0, 0.0).astype(jnp.bfloat16)
    loads[2].wait()
    for blocks in (part, part_in):
        blocks[NZ:] = jnp.zeros_like(blocks[NZ:])

    def arrived(n):
        for e in range(1, NX):
            px(n, e).wait_recv()

    def two(j, _):
        older, old = (2 * j + NZ) % (NZ + 2), (2 * j + NZ + 1) % (NZ + 2)

        @pl.when(j == 1)
        def _():
            hop(3)

        @pl.when(j > 0)
        def _():
            arrived(older)

        attention(2 * j + 1, j + 1 + j // 3, 1, 2 * j, 0, older)

        @pl.when(j == 0)
        def _():
            hop(2)

        @pl.when(j == 1)
        def _():
            hop(4)

        @pl.when(j == 2)
        def _():
            pz(2).start()

        @pl.when(j == 3)
        def _():
            pz(4).start()

        @pl.when(j > 0)
        def _():
            arrived(old)

        @pl.when(j < 3)
        def _():
            attention(2 * j + 2, 7 - j - j // 2, 0, 2 * j + 1, 1, old)

        @pl.when(j == 3)
        def _():
            attention(None, None, None, 2 * j + 1, 1, old)
            pz(5).start()

        @pl.when(j == 1)
        def _():
            pz(1).start()

        @pl.when(j == 2)
        def _():
            pz(3).start()

        return 0

    lax.fori_loop(0, NZ // 2, two, 0)

    def last(n, _):
        arrived(n)
        over_x(n)

        @pl.when(n == NZ - 2)
        def _():
            pz(NZ - 2).start()

        @pl.when(n == NZ - 1)
        def _():
            pz(NZ - 1).start()

        return 0

    lax.fori_loop(NZ - 2, NZ, last, 0)

    for n in range(1, NZ):
        pz(n).wait_recv()
    outs = [lambda h: zpart[0, :, h * HEAD : (h + 1) * HEAD]]
    outs += [lambda h, n=n: z_in[n, :, h * HEAD : (h + 1) * HEAD] for n in range(1, NZ)]
    merged, _ = merge([zpart[0, :, COLS:WIDE]] + [z_in[n, :, COLS:WIDE] for n in range(1, NZ)], outs)
    for h in range(HEADS):
        att[x, block(z), h * HEAD : (h + 1) * HEAD] = merged[h]

    near = (0, 1, 7, 2, 6, 3, 5, 4)
    for e in (1, 3, 2):
        ax(0, e).start()
    for d in near[1:]:
        az(d).start()
    for d in near[1:]:
        az(d).wait_recv()
        for e in (1, 3, 2):
            ax(d, e).start()

    def project(source):
        rows = pl.ds(pl.multiple_of(source * CHUNK, CHUNK), CHUNK)
        t = dot(att[source], w_buf[...]).astype(jnp.bfloat16)
        terms[rows] = t
        for j in range(CHUNK // SHARE):
            owner = source * (CHUNK // SHARE) + j
            t_out[owner] = t[j * SHARE : (j + 1) * SHARE]

            @pl.when(owner != kvh)
            def _():
                tk((owner + NK - kvh) % NK).start()

    project(x)
    for e in (1, 3, 2):
        for d in near:
            ax(d, e).wait_recv()
        project((x + NX - e) % NX)

    partners = dot(pairs[...], terms[...]).astype(jnp.bfloat16)
    for i in range(NK):
        p_out[i] = partners[i * SHARE : (i + 1) * SHARE]
    for d in range(1, NK):
        pk(d).start()
    t_in[kvh] = t_out[kvh]
    p_in[kvh] = p_out[kvh]

    def total(ref):
        t = ref[0].astype(jnp.float32)
        for i in range(1, NK):
            t = t + ref[i].astype(jnp.float32)
        return t.astype(jnp.bfloat16)

    for d in range(1, NK):
        tk(d).wait_recv()
    total_ref[:, 0:OUT] = total(t_in)
    for d in range(1, NK):
        pk(d).wait_recv()
    total_ref[:, OUT:] = total(p_in)

    for n in range(NZ):
        for e in range(1, NX):
            fq(n, e).wait_send()
            px(n, e).wait_send()
            ax(n, e).wait_send()
    for k in range(1, NZ // 2 + 1):
        up(k).wait_send()
        if k < NZ // 2:
            down(k).wait_send()
    for d in range(1, NZ):
        pz(d).wait_send()
        az(d).wait_send()
    for d in range(1, NK):
        tk(d).wait_send()
        pk(d).wait_send()


def per_device(queries, keys, values, out_weight, positions, partner):
    bf, f32 = jnp.bfloat16, jnp.float32
    vmem = pl.BlockSpec(memory_space=pltpu.VMEM)
    any_ = pl.BlockSpec(memory_space=pl.ANY)
    dma = pltpu.SemaphoreType.DMA
    total = pl.pallas_call(
        kernel,
        out_shape=jax.ShapeDtypeStruct((SHARE, 2 * OUT), bf),
        in_specs=[vmem, any_, any_, any_, pl.BlockSpec(memory_space=pltpu.SMEM), vmem],
        out_specs=vmem,
        scratch_shapes=[
            pltpu.VMEM((LENGTH, HEAD), bf),
            pltpu.VMEM((LENGTH, HEAD), bf),
            pltpu.VMEM((COLS, OUT), bf),
            pltpu.VMEM((LENGTH, 2 * HEAD), bf),
            pltpu.VMEM((ROWS, LENGTH), f32),
            pltpu.VMEM((ROWS, LENGTH), f32),
            pltpu.VMEM((2, ROWS, 128), f32),
            pltpu.VMEM((NZ, SLAB, WIDE), bf),
            pltpu.VMEM((NZ + 2, SLAB, WIDE), bf),
            pltpu.VMEM((NZ + 2, NX - 1, TOK, WIDE), bf),
            pltpu.VMEM((NZ + 2, TOK, WIDE), bf),
            pltpu.VMEM((NZ, TOK, WIDE), bf),
            pltpu.VMEM((NX, CHUNK, COLS), bf),
            pltpu.VMEM((TOKENS, TOKENS), bf),
            pltpu.VMEM((TOKENS, OUT), bf),
            pltpu.VMEM((NK, SHARE, OUT), bf),
            pltpu.VMEM((NK, SHARE, OUT), bf),
            pltpu.VMEM((NK, SHARE, OUT), bf),
            pltpu.VMEM((NK, SHARE, OUT), bf),
            dma((3,)),
            dma((NZ, NX - 1)), dma((NZ, NX - 1)),
            dma((4,)), dma((4,)), dma((4,)), dma((4,)),
            dma((NZ, NX - 1)), dma((NZ, NX - 1)),
            dma((NZ - 1,)), dma((NZ - 1,)),
            dma((NZ - 1,)), dma((NZ - 1,)),
            dma((NZ, NX - 1)), dma((NZ, NX - 1)),
            dma((NK - 1,)), dma((NK - 1,)), dma((NK - 1,)), dma((NK - 1,)),
        ],
        compiler_params=pltpu.CompilerParams(
            collective_id=0, has_side_effects=True, vmem_limit_bytes=56 * 2**20),
    )(queries, keys, values, out_weight, positions, partner.reshape(1, TOKENS))
    mixed, other = total[:, 0:OUT], total[:, OUT:]
    return mixed, (mixed.astype(f32) - other.astype(f32)).astype(bf)


def solution(mesh):
    placed = (P("seq", "kvh"), P("seq", "kvh"), P("seq", "kvh"), P("kvh", "seq"), P("seq"), P())
    return jax.shard_map(
        per_device,
        mesh=mesh,
        in_specs=placed,
        out_specs=(P("kvh", "seq"), P("kvh", "seq")),
        check_vma=False,
    )
```

```python
import math

import jax
import jax.numpy as jnp
from jax import lax
from jax.experimental import pallas as pl
from jax.experimental.pallas import tpu as pltpu
from jax.sharding import PartitionSpec as P

MESH = pl.DeviceIdType.MESH

HEADS = 8
HEAD = 128
NX, NZ, NK = 4, 8, 8
LENGTH = 4096
TOK = 16
CHUNK = NZ * TOK
TOKENS = NX * CHUNK
COLS = HEADS * HEAD
WIDE = COLS + 128
OUT = 256
SHARE = TOKENS // NK

SLAB = NX * TOK
ROWS = HEADS * SLAB
STEP = 1024

LOW = -1e30
SCALE2 = math.log2(math.e) / math.sqrt(HEAD)


def dot(a, b):
    return lax.dot_general(a, b, (((1,), (0,)), ((), ())), preferred_element_type=jnp.float32)


def dot_t(a, b):
    return lax.dot_general(a, b, (((1,), (1,)), ((), ())), preferred_element_type=jnp.float32)


def spread(t):
    lane = lax.broadcasted_iota(jnp.int32, t.shape, 1)
    t = jnp.where(lane < 8, t, 0.0)
    t = t + pltpu.roll(t, 8, 1) + pltpu.roll(t, 16, 1)
    first = t.astype(jnp.bfloat16).astype(jnp.float32)
    rest = t - first
    second = rest.astype(jnp.bfloat16).astype(jnp.float32)
    third = rest - second
    return jnp.where(lane < 8, first, jnp.where(lane < 16, second, third)).astype(jnp.bfloat16)


def gathered(t):
    t = t.astype(jnp.float32)
    return t + pltpu.roll(t, 120, 1) + pltpu.roll(t, 112, 1)


def merge(tiles, outs):
    logs = [gathered(t) for t in tiles]
    top = logs[0]
    for u in logs[1:]:
        top = jnp.maximum(top, u)
    shares = [jnp.exp2(u - top) for u in logs]
    total = shares[0]
    for w in shares[1:]:
        total = total + w
    inverse = 1.0 / total
    shares = [w * inverse for w in shares]
    merged = []
    for h in range(HEADS):
        acc = None
        for w, o in zip(shares, outs):
            term = w[:, h : h + 1] * o(h).astype(jnp.float32)
            acc = term if acc is None else acc + term
        merged.append(acc.astype(jnp.bfloat16))
    return merged, top + jnp.log2(total)


def kernel(
    q_ref, k_ref, v_ref, w_ref, pos_ref, partner_ref, total_ref,
    k_buf, v_buf, w_buf, vp, s0, s1, run, q_all, part, part_in, zpart, z_in, att, pairs, terms, t_out, t_in, p_out, p_in,
    local_sem, fq_send, fq_recv, up_send, up_recv, down_send, down_recv, px_send, px_recv, pz_send, pz_recv,
    az_send, az_recv, ax_send, ax_recv, t_send, t_recv, p_send, p_recv,
):
    seq = lax.axis_index("seq")
    kvh = lax.axis_index("kvh")
    x = seq // NZ
    z = seq % NZ

    def x_peer(d):
        return (((x + d) % NX) * NZ + z, kvh)

    def z_peer(d):
        return (x * NZ + (z + d) % NZ, kvh)

    def k_peer(d):
        return (seq, (kvh + d) % NK)

    def block(i):
        return pl.ds(pl.multiple_of(i * TOK, TOK), TOK)

    def remote(src, dst, send, recv, peer):
        return pltpu.make_async_remote_copy(
            src_ref=src, dst_ref=dst, send_sem=send, recv_sem=recv, device_id=peer, device_id_type=MESH)

    loads = [
        pltpu.make_async_copy(src, dst, local_sem.at[i])
        for i, (src, dst) in enumerate(((k_ref, k_buf), (v_ref, v_buf), (w_ref, w_buf)))
    ]
    for c in loads:
        c.start()

    barrier = pltpu.get_barrier_semaphore()
    for d in range(1, NX):
        pl.semaphore_signal(barrier, inc=1, device_id=x_peer(d), device_id_type=MESH)
    for d in (1, NZ - 1):
        pl.semaphore_signal(barrier, inc=1, device_id=z_peer(d), device_id_type=MESH)
    for d in range(1, NK):
        pl.semaphore_signal(barrier, inc=1, device_id=k_peer(d), device_id_type=MESH)

    row = lax.broadcasted_iota(jnp.int32, (TOK, 128), 0)
    lane = lax.broadcasted_iota(jnp.int32, (TOK, 128), 1)
    counts = jnp.zeros((TOK, 128), jnp.int32)
    for i in range(TOK):
        counts = jnp.where(row == i, pos_ref[i], counts)
    high = lax.shift_right_logical(counts, 12)
    middle = lax.bitwise_and(lax.shift_right_logical(counts, 4), 255)
    low = lax.bitwise_and(counts, 15)
    counts = jnp.where(lane == 0, high, jnp.where(lane == 1, middle, low))
    q_all[z, block(x), 0:COLS] = q_ref[...]
    q_all[z, block(x), COLS:WIDE] = counts.astype(jnp.float32).astype(jnp.bfloat16)

    pl.semaphore_wait(barrier, NX + NK)

    def up(k):
        here = q_all.at[(z + NZ + 1 - k) % NZ, block(x)]
        return remote(here, here, up_send.at[k - 1], up_recv.at[k - 1], z_peer(1))

    def down(k):
        here = q_all.at[(z + k - 1) % NZ, block(x)]
        return remote(here, here, down_send.at[k - 1], down_recv.at[k - 1], z_peer(NZ - 1))

    def fq(dz, e):
        here = q_all.at[(z + dz) % NZ, block(x)]
        return remote(here, here, fq_send.at[dz, e - 1], fq_recv.at[dz, e - 1], x_peer(e))

    def hop(k):
        up(k).wait_recv()
        if k < NZ // 2:
            down(k).wait_recv()
            up(k + 1).start()
        if k + 1 < NZ // 2:
            down(k + 1).start()
        for e in (1, 3, 2):
            fq(NZ - k, e).start()
            if k < NZ // 2:
                fq(k, e).start()

    def px(n, d):
        return remote(part.at[n, block((x + d) % NX)], part_in.at[n, d - 1],
                      px_send.at[n, d - 1], px_recv.at[n, d - 1], x_peer(d))

    order = (0, 1, 7, 2, 6, 3, 4, 5)

    def pz(n):
        return remote(zpart.at[n], z_in.at[n], pz_send.at[n - 1], pz_recv.at[n - 1], z_peer(order[n]))

    def az(d):
        here = att.at[x, block(z)]
        return remote(here, here, az_send.at[d - 1], az_recv.at[d - 1], z_peer(d))

    def ax(d, e):
        here = att.at[x, block((z + NZ - d) % NZ)]
        return remote(here, here, ax_send.at[d, e - 1], ax_recv.at[d, e - 1], x_peer(e))

    def tk(d):
        return remote(t_out.at[(kvh + d) % NK], t_in.at[kvh], t_send.at[d - 1], t_recv.at[d - 1], k_peer(d))

    def pk(d):
        return remote(p_out.at[(kvh + d) % NK], p_in.at[kvh], p_send.at[d - 1], p_recv.at[d - 1], k_peer(d))

    up(1).start()
    down(1).start()
    for e in (1, 3, 2):
        fq(0, e).start()

    loads[1].wait()
    vp[:, 0:HEAD] = v_buf[...]
    vp[:, HEAD:] = jnp.where(lax.broadcasted_iota(jnp.int32, (LENGTH, 128), 1) == 0, 1.0, 0.0).astype(jnp.bfloat16)
    loads[0].wait()

    start = seq * LENGTH
    run_of = (run.at[0], run.at[1])

    def attention(a, dz, a_slot, b, b_slot, done=None):
        if a is not None:
            for e in (1, 3, 2):
                fq(dz, e).wait_recv()
            a_z = (z + dz) % NZ
            q = jnp.concatenate([q_all[a_z, :, h * HEAD : (h + 1) * HEAD] for h in range(HEADS)], axis=0)
            c = q_all[a_z, :, COLS:WIDE].astype(jnp.float32)
            count = (c[:, 0:1] * 4096.0 + c[:, 1:2] * 16.0 + c[:, 2:3]).astype(jnp.int32) - start
            a_s = (s0, s1)[a_slot]
            a_run = None
        if b is not None:
            b_s = (s0, s1)[b_slot]
            top = jnp.maximum(jnp.max(run_of[b_slot][...], axis=1, keepdims=True), -1e29)
            total = None
        for i in range(LENGTH // STEP):
            cols = pl.ds(i * STEP, STEP)
            if a is not None:
                s = dot_t(q, k_buf[cols, :]) * SCALE2
                seen = (i * STEP + lax.broadcasted_iota(jnp.int32, (SLAB, STEP), 1)) < count
                s = jnp.where(seen[None], s.reshape(HEADS, SLAB, STEP), LOW).reshape(ROWS, STEP)
                a_s[:, cols] = s
                for j in range(STEP // 128):
                    m = s[:, j * 128 : (j + 1) * 128]
                    a_run = m if a_run is None else jnp.maximum(a_run, m)
            if b is not None:
                o = dot(jnp.exp2(b_s[:, cols] - top).astype(jnp.bfloat16), vp[cols, :])
                total = o if total is None else total + o
            if done is not None and i == 1:
                over_x(done)
        if a is not None:
            run_of[a_slot][...] = a_run
        if b is not None:
            weight = total[:, HEAD : HEAD + 1]
            some = weight > 0.0
            weight = jnp.where(some, weight, 1.0)
            out = total[:, 0:HEAD] / weight
            log = jnp.where(some, top + jnp.log2(weight), LOW)
            lanes = lax.broadcasted_iota(jnp.int32, (SLAB, 128), 1)
            tile = jnp.zeros((SLAB, 128), jnp.float32)
            for h in range(HEADS):
                part[b, :, h * HEAD : (h + 1) * HEAD] = out[h * SLAB : (h + 1) * SLAB].astype(jnp.bfloat16)
                tile = jnp.where(lanes == h, log[h * SLAB : (h + 1) * SLAB], tile)
            part[b, :, COLS:WIDE] = spread(tile)
            for d in range(1, NX):
                px(b, d).start()

    def over_x(n):
        outs = [lambda h: part[n, block(x), h * HEAD : (h + 1) * HEAD]]
        outs += [lambda h, d=d: part_in[n, d, :, h * HEAD : (h + 1) * HEAD] for d in range(NX - 1)]
        tiles = [part[n, block(x), COLS:WIDE]] + [part_in[n, d, :, COLS:WIDE] for d in range(NX - 1)]
        merged, log = merge(tiles, outs)
        for h in range(HEADS):
            zpart[n, :, h * HEAD : (h + 1) * HEAD] = merged[h]
        zpart[n, :, COLS:WIDE] = spread(log)

    hop(1)
    attention(0, 0, 0, None, None)
    pairs[...] = jnp.where(
        lax.broadcasted_iota(jnp.int32, (TOKENS, TOKENS), 0) == partner_ref[...], 1.0, 0.0).astype(jnp.bfloat16)
    loads[2].wait()
    for blocks in (part, part_in):
        blocks[NZ:] = jnp.zeros_like(blocks[NZ:])
    hop(2)

    def arrived(n):
        for e in range(1, NX):
            px(n, e).wait_recv()

    def two(j, _):
        older, old = (2 * j + NZ) % (NZ + 3), (2 * j + NZ + 1) % (NZ + 3)

        @pl.when(j == 1)
        def _():
            hop(4)

        @pl.when(j > 1)
        def _():
            arrived(older)

        attention(2 * j + 1, j + 1 + j // 3, 1, 2 * j, 0, older)

        @pl.when(j == 0)
        def _():
            hop(3)

        @pl.when(j == 2)
        def _():
            pz(1).start()

        @pl.when(j == 3)
        def _():
            pz(3).start()

        @pl.when(j > 0)
        def _():
            arrived(old)

        @pl.when(j < 3)
        def _():
            attention(2 * j + 2, 7 - j - j // 2, 0, 2 * j + 1, 1, old)

        @pl.when(j == 3)
        def _():
            attention(None, None, None, 2 * j + 1, 1, old)
            pz(4).start()

        @pl.when(j == 2)
        def _():
            pz(2).start()

        return 0

    lax.fori_loop(0, NZ // 2, two, 0)

    def last(n, _):
        arrived(n)
        over_x(n)

        for m in range(NZ - 3, NZ):

            @pl.when(n == m)
            def _():
                pz(m).start()

        return 0

    lax.fori_loop(NZ - 3, NZ, last, 0)

    for n in range(1, NZ):
        pz(n).wait_recv()
    outs = [lambda h: zpart[0, :, h * HEAD : (h + 1) * HEAD]]
    outs += [lambda h, n=n: z_in[n, :, h * HEAD : (h + 1) * HEAD] for n in range(1, NZ)]
    merged, _ = merge([zpart[0, :, COLS:WIDE]] + [z_in[n, :, COLS:WIDE] for n in range(1, NZ)], outs)
    for h in range(HEADS):
        att[x, block(z), h * HEAD : (h + 1) * HEAD] = merged[h]

    near = (0, 1, 7, 2, 6, 3, 5, 4)
    for e in (1, 3, 2):
        ax(0, e).start()
    for d in near[1:]:
        az(d).start()
    for d in near[1:]:
        az(d).wait_recv()
        for e in (1, 3, 2):
            ax(d, e).start()

    def project(source):
        rows = pl.ds(pl.multiple_of(source * CHUNK, CHUNK), CHUNK)
        t = dot(att[source], w_buf[...]).astype(jnp.bfloat16)
        terms[rows] = t
        for j in range(CHUNK // SHARE):
            owner = source * (CHUNK // SHARE) + j
            t_out[owner] = t[j * SHARE : (j + 1) * SHARE]

            @pl.when(owner != kvh)
            def _():
                tk((owner + NK - kvh) % NK).start()

    project(x)
    for e in (1, 3, 2):
        for d in near:
            ax(d, e).wait_recv()
        project((x + NX - e) % NX)

    partners = dot(pairs[...], terms[...]).astype(jnp.bfloat16)
    for i in range(NK):
        p_out[i] = partners[i * SHARE : (i + 1) * SHARE]
    for d in range(1, NK):
        pk(d).start()
    t_in[kvh] = t_out[kvh]
    p_in[kvh] = p_out[kvh]

    def total(ref):
        t = ref[0].astype(jnp.float32)
        for i in range(1, NK):
            t = t + ref[i].astype(jnp.float32)
        return t.astype(jnp.bfloat16)

    for d in range(1, NK):
        tk(d).wait_recv()
    total_ref[:, 0:OUT] = total(t_in)
    for d in range(1, NK):
        pk(d).wait_recv()
    total_ref[:, OUT:] = total(p_in)

    for n in range(NZ):
        for e in range(1, NX):
            fq(n, e).wait_send()
            px(n, e).wait_send()
            ax(n, e).wait_send()
    for k in range(1, NZ // 2 + 1):
        up(k).wait_send()
        if k < NZ // 2:
            down(k).wait_send()
    for d in range(1, NZ):
        pz(d).wait_send()
        az(d).wait_send()
    for d in range(1, NK):
        tk(d).wait_send()
        pk(d).wait_send()


def per_device(queries, keys, values, out_weight, positions, partner):
    bf, f32 = jnp.bfloat16, jnp.float32
    vmem = pl.BlockSpec(memory_space=pltpu.VMEM)
    any_ = pl.BlockSpec(memory_space=pl.ANY)
    dma = pltpu.SemaphoreType.DMA
    total = pl.pallas_call(
        kernel,
        out_shape=jax.ShapeDtypeStruct((SHARE, 2 * OUT), bf),
        in_specs=[vmem, any_, any_, any_, pl.BlockSpec(memory_space=pltpu.SMEM), vmem],
        out_specs=vmem,
        scratch_shapes=[
            pltpu.VMEM((LENGTH, HEAD), bf),
            pltpu.VMEM((LENGTH, HEAD), bf),
            pltpu.VMEM((COLS, OUT), bf),
            pltpu.VMEM((LENGTH, 2 * HEAD), bf),
            pltpu.VMEM((ROWS, LENGTH), f32),
            pltpu.VMEM((ROWS, LENGTH), f32),
            pltpu.VMEM((2, ROWS, 128), f32),
            pltpu.VMEM((NZ, SLAB, WIDE), bf),
            pltpu.VMEM((NZ + 3, SLAB, WIDE), bf),
            pltpu.VMEM((NZ + 3, NX - 1, TOK, WIDE), bf),
            pltpu.VMEM((NZ + 3, TOK, WIDE), bf),
            pltpu.VMEM((NZ, TOK, WIDE), bf),
            pltpu.VMEM((NX, CHUNK, COLS), bf),
            pltpu.VMEM((TOKENS, TOKENS), bf),
            pltpu.VMEM((TOKENS, OUT), bf),
            pltpu.VMEM((NK, SHARE, OUT), bf),
            pltpu.VMEM((NK, SHARE, OUT), bf),
            pltpu.VMEM((NK, SHARE, OUT), bf),
            pltpu.VMEM((NK, SHARE, OUT), bf),
            dma((3,)),
            dma((NZ, NX - 1)), dma((NZ, NX - 1)),
            dma((4,)), dma((4,)), dma((4,)), dma((4,)),
            dma((NZ, NX - 1)), dma((NZ, NX - 1)),
            dma((NZ - 1,)), dma((NZ - 1,)),
            dma((NZ - 1,)), dma((NZ - 1,)),
            dma((NZ, NX - 1)), dma((NZ, NX - 1)),
            dma((NK - 1,)), dma((NK - 1,)), dma((NK - 1,)), dma((NK - 1,)),
        ],
        compiler_params=pltpu.CompilerParams(
            collective_id=0, has_side_effects=True, vmem_limit_bytes=56 * 2**20),
    )(queries, keys, values, out_weight, positions, partner.reshape(1, TOKENS))
    mixed, other = total[:, 0:OUT], total[:, OUT:]
    return mixed, (mixed.astype(f32) - other.astype(f32)).astype(bf)


def solution(mesh):
    placed = (P("seq", "kvh"), P("seq", "kvh"), P("seq", "kvh"), P("kvh", "seq"), P("seq"), P())
    return jax.shard_map(
        per_device,
        mesh=mesh,
        in_specs=placed,
        out_specs=(P("kvh", "seq"), P("kvh", "seq")),
        check_vma=False,
    )
```

```python
import math

import jax
import jax.numpy as jnp
from jax import lax
from jax.experimental import pallas as pl
from jax.experimental.pallas import tpu as pltpu
from jax.sharding import PartitionSpec as P

MESH = pl.DeviceIdType.MESH

HEADS = 8
HEAD = 128
NX, NZ, NK = 4, 8, 8
LENGTH = 4096
TOK = 16
CHUNK = NZ * TOK
TOKENS = NX * CHUNK
COLS = HEADS * HEAD
WIDE = COLS + 128
OUT = 256
SHARE = TOKENS // NK

SLAB = NX * TOK
ROWS = HEADS * SLAB
STEP = 1024

LOW = -1e30
SCALE2 = math.log2(math.e) / math.sqrt(HEAD)


def dot(a, b):
    return lax.dot_general(a, b, (((1,), (0,)), ((), ())), preferred_element_type=jnp.float32)


def dot_t(a, b):
    return lax.dot_general(a, b, (((1,), (1,)), ((), ())), preferred_element_type=jnp.float32)


def spread(t):
    lane = lax.broadcasted_iota(jnp.int32, t.shape, 1)
    t = jnp.where(lane < 8, t, 0.0)
    t = t + pltpu.roll(t, 8, 1) + pltpu.roll(t, 16, 1)
    first = t.astype(jnp.bfloat16).astype(jnp.float32)
    rest = t - first
    second = rest.astype(jnp.bfloat16).astype(jnp.float32)
    third = rest - second
    return jnp.where(lane < 8, first, jnp.where(lane < 16, second, third)).astype(jnp.bfloat16)


def gathered(t):
    t = t.astype(jnp.float32)
    return t + pltpu.roll(t, 120, 1) + pltpu.roll(t, 112, 1)


def merge(tiles, outs):
    logs = [gathered(t) for t in tiles]
    top = logs[0]
    for u in logs[1:]:
        top = jnp.maximum(top, u)
    shares = [jnp.exp2(u - top) for u in logs]
    total = shares[0]
    for w in shares[1:]:
        total = total + w
    inverse = 1.0 / total
    shares = [w * inverse for w in shares]
    merged = []
    for h in range(HEADS):
        acc = None
        for w, o in zip(shares, outs):
            term = w[:, h : h + 1] * o(h).astype(jnp.float32)
            acc = term if acc is None else acc + term
        merged.append(acc.astype(jnp.bfloat16))
    return merged, top + jnp.log2(total)


def kernel(
    q_ref, k_ref, v_ref, w_ref, pos_ref, partner_ref, total_ref,
    k_buf, v_buf, w_buf, vp, s0, s1, run, q_all, part, part_in, zpart, z_in, att, pairs, terms, t_out, t_in, p_out, p_in,
    local_sem, fq_send, fq_recv, side_send, side_recv, up_send, up_recv, down_send, down_recv, px_send, px_recv, pz_send, pz_recv,
    az_send, az_recv, ax_send, ax_recv, t_send, t_recv, p_send, p_recv,
):
    seq = lax.axis_index("seq")
    kvh = lax.axis_index("kvh")
    x = seq // NZ
    z = seq % NZ

    def x_peer(d):
        return (((x + d) % NX) * NZ + z, kvh)

    def z_peer(d):
        return (x * NZ + (z + d) % NZ, kvh)

    def k_peer(d):
        return (seq, (kvh + d) % NK)

    def block(i):
        return pl.ds(pl.multiple_of(i * TOK, TOK), TOK)

    def remote(src, dst, send, recv, peer):
        return pltpu.make_async_remote_copy(
            src_ref=src, dst_ref=dst, send_sem=send, recv_sem=recv, device_id=peer, device_id_type=MESH)

    loads = [
        pltpu.make_async_copy(src, dst, local_sem.at[i])
        for i, (src, dst) in enumerate(((k_ref, k_buf), (v_ref, v_buf), (w_ref, w_buf)))
    ]
    for c in loads:
        c.start()

    barrier = pltpu.get_barrier_semaphore()
    for d in range(1, NX):
        pl.semaphore_signal(barrier, inc=1, device_id=x_peer(d), device_id_type=MESH)
    for d in (1, NZ - 1):
        pl.semaphore_signal(barrier, inc=1, device_id=z_peer(d), device_id_type=MESH)
    for d in range(1, NK):
        pl.semaphore_signal(barrier, inc=1, device_id=k_peer(d), device_id_type=MESH)

    row = lax.broadcasted_iota(jnp.int32, (TOK, 128), 0)
    lane = lax.broadcasted_iota(jnp.int32, (TOK, 128), 1)
    counts = jnp.zeros((TOK, 128), jnp.int32)
    for i in range(TOK):
        counts = jnp.where(row == i, pos_ref[i], counts)
    high = lax.shift_right_logical(counts, 12)
    middle = lax.bitwise_and(lax.shift_right_logical(counts, 4), 255)
    low = lax.bitwise_and(counts, 15)
    counts = jnp.where(lane == 0, high, jnp.where(lane == 1, middle, low))
    q_all[z, block(x), 0:COLS] = q_ref[...]
    q_all[z, block(x), COLS:WIDE] = counts.astype(jnp.float32).astype(jnp.bfloat16)

    pl.semaphore_wait(barrier, NX + NK)

    def up(k):
        here = q_all.at[(z + NZ + 1 - k) % NZ, block(x)]
        return remote(here, here, up_send.at[k - 1], up_recv.at[k - 1], z_peer(1))

    def down(k):
        here = q_all.at[(z + k - 1) % NZ, block(x)]
        return remote(here, here, down_send.at[k - 1], down_recv.at[k - 1], z_peer(NZ - 1))

    def fq(dz, e):
        here = q_all.at[(z + dz) % NZ, block(x)]
        return remote(here, here, fq_send.at[dz, e - 1], fq_recv.at[dz, e - 1], x_peer(e))

    def side(e, way):
        here = q_all.at[z, block((x + e) % NX)]
        return remote(here, here, side_send.at[way, e - 1], side_recv.at[way, e - 1], z_peer((1, NZ - 1)[way]))

    def hop(k):
        up(k).wait_recv()
        if k < NZ // 2:
            down(k).wait_recv()
            up(k + 1).start()
        if k + 1 < NZ // 2:
            down(k + 1).start()
        for e in (1, 3, 2):
            if k > 1:
                fq(NZ - k, e).start()
            if 1 < k < NZ // 2:
                fq(k, e).start()

    def px(n, d):
        return remote(part.at[n, block((x + d) % NX)], part_in.at[n, d - 1],
                      px_send.at[n, d - 1], px_recv.at[n, d - 1], x_peer(d))

    order = (0, 1, 7, 2, 6, 3, 4, 5)

    def pz(n):
        return remote(zpart.at[n], z_in.at[n], pz_send.at[n - 1], pz_recv.at[n - 1], z_peer(order[n]))

    def az(d):
        here = att.at[x, block(z)]
        return remote(here, here, az_send.at[d - 1], az_recv.at[d - 1], z_peer(d))

    def ax(d, e):
        here = att.at[x, block((z + NZ - d) % NZ)]
        return remote(here, here, ax_send.at[d, e - 1], ax_recv.at[d, e - 1], x_peer(e))

    def tk(d):
        return remote(t_out.at[(kvh + d) % NK], t_in.at[kvh], t_send.at[d - 1], t_recv.at[d - 1], k_peer(d))

    def pk(d):
        return remote(p_out.at[(kvh + d) % NK], p_in.at[kvh], p_send.at[d - 1], p_recv.at[d - 1], k_peer(d))

    up(1).start()
    down(1).start()
    for e in (1, 3, 2):
        fq(0, e).start()

    loads[1].wait()
    vp[:, 0:HEAD] = v_buf[...]
    vp[:, HEAD:] = jnp.where(lax.broadcasted_iota(jnp.int32, (LENGTH, 128), 1) == 0, 1.0, 0.0).astype(jnp.bfloat16)
    loads[0].wait()

    start = seq * LENGTH
    run_of = (run.at[0], run.at[1])

    def attention(a, dz, a_slot, b, b_slot, done=None):
        if a is not None:
            a_z = (z + dz) % NZ
            q = jnp.concatenate([q_all[a_z, :, h * HEAD : (h + 1) * HEAD] for h in range(HEADS)], axis=0)
            c = q_all[a_z, :, COLS:WIDE].astype(jnp.float32)
            count = (c[:, 0:1] * 4096.0 + c[:, 1:2] * 16.0 + c[:, 2:3]).astype(jnp.int32) - start
            a_s = (s0, s1)[a_slot]
            a_run = None
        if b is not None:
            b_s = (s0, s1)[b_slot]
            top = jnp.maximum(jnp.max(run_of[b_slot][...], axis=1, keepdims=True), -1e29)
            total = None
        for i in range(LENGTH // STEP):
            cols = pl.ds(i * STEP, STEP)
            if a is not None:
                s = dot_t(q, k_buf[cols, :]) * SCALE2
                seen = (i * STEP + lax.broadcasted_iota(jnp.int32, (SLAB, STEP), 1)) < count
                s = jnp.where(seen[None], s.reshape(HEADS, SLAB, STEP), LOW).reshape(ROWS, STEP)
                a_s[:, cols] = s
                for j in range(STEP // 128):
                    m = s[:, j * 128 : (j + 1) * 128]
                    a_run = m if a_run is None else jnp.maximum(a_run, m)
            if b is not None:
                o = dot(jnp.exp2(b_s[:, cols] - top).astype(jnp.bfloat16), vp[cols, :])
                total = o if total is None else total + o
            if done is not None and i == 1:
                over_x(done)
        if a is not None:
            run_of[a_slot][...] = a_run
        if b is not None:
            weight = total[:, HEAD : HEAD + 1]
            some = weight > 0.0
            weight = jnp.where(some, weight, 1.0)
            out = total[:, 0:HEAD] / weight
            log = jnp.where(some, top + jnp.log2(weight), LOW)
            lanes = lax.broadcasted_iota(jnp.int32, (SLAB, 128), 1)
            tile = jnp.zeros((SLAB, 128), jnp.float32)
            for h in range(HEADS):
                part[b, :, h * HEAD : (h + 1) * HEAD] = out[h * SLAB : (h + 1) * SLAB].astype(jnp.bfloat16)
                tile = jnp.where(lanes == h, log[h * SLAB : (h + 1) * SLAB], tile)
            part[b, :, COLS:WIDE] = spread(tile)
            for d in range(1, NX):
                px(b, d).start()

    def over_x(n):
        outs = [lambda h: part[n, block(x), h * HEAD : (h + 1) * HEAD]]
        outs += [lambda h, d=d: part_in[n, d, :, h * HEAD : (h + 1) * HEAD] for d in range(NX - 1)]
        tiles = [part[n, block(x), COLS:WIDE]] + [part_in[n, d, :, COLS:WIDE] for d in range(NX - 1)]
        merged, log = merge(tiles, outs)
        for h in range(HEADS):
            zpart[n, :, h * HEAD : (h + 1) * HEAD] = merged[h]
        zpart[n, :, COLS:WIDE] = spread(log)

    for e in (1, 3, 2):
        fq(0, e).wait_recv()
        side(NX - e, 0).start()
        side(NX - e, 1).start()
    hop(1)
    attention(0, 0, 0, None, None)
    pairs[...] = jnp.where(
        lax.broadcasted_iota(jnp.int32, (TOKENS, TOKENS), 0) == partner_ref[...], 1.0, 0.0).astype(jnp.bfloat16)
    loads[2].wait()
    for blocks in (part, part_in):
        blocks[NZ:] = jnp.zeros_like(blocks[NZ:])
    hop(2)

    def arrived(n):
        for e in range(1, NX):
            px(n, e).wait_recv()

    def two(j, _):
        older, old = (2 * j + NZ) % (NZ + 3), (2 * j + NZ + 1) % (NZ + 3)

        @pl.when(j == 1)
        def _():
            hop(4)

        @pl.when(j > 1)
        def _():
            arrived(older)

        @pl.when(j == 0)
        def _():
            for e in range(1, NX):
                side(e, 1).wait_recv()

        @pl.when(j > 0)
        def _():
            for e in range(1, NX):
                fq(j + 1 + j // 3, e).wait_recv()

        attention(2 * j + 1, j + 1 + j // 3, 1, 2 * j, 0, older)

        @pl.when(j == 0)
        def _():
            hop(3)

        @pl.when(j == 2)
        def _():
            pz(1).start()

        @pl.when(j == 3)
        def _():
            pz(3).start()

        @pl.when(j > 0)
        def _():
            arrived(old)

        @pl.when(j == 0)
        def _():
            for e in range(1, NX):
                side(e, 0).wait_recv()

        @pl.when(j * (3 - j) > 0)
        def _():
            for e in range(1, NX):
                fq(7 - j - j // 2, e).wait_recv()

        @pl.when(j < 3)
        def _():
            attention(2 * j + 2, 7 - j - j // 2, 0, 2 * j + 1, 1, old)

        @pl.when(j == 3)
        def _():
            attention(None, None, None, 2 * j + 1, 1, old)
            pz(4).start()

        @pl.when(j == 2)
        def _():
            pz(2).start()

        return 0

    lax.fori_loop(0, NZ // 2, two, 0)

    def last(n, _):
        arrived(n)
        over_x(n)

        for m in range(NZ - 3, NZ):

            @pl.when(n == m)
            def _():
                pz(m).start()

        return 0

    lax.fori_loop(NZ - 3, NZ, last, 0)

    for n in range(1, NZ):
        pz(n).wait_recv()
    outs = [lambda h: zpart[0, :, h * HEAD : (h + 1) * HEAD]]
    outs += [lambda h, n=n: z_in[n, :, h * HEAD : (h + 1) * HEAD] for n in range(1, NZ)]
    merged, _ = merge([zpart[0, :, COLS:WIDE]] + [z_in[n, :, COLS:WIDE] for n in range(1, NZ)], outs)
    for h in range(HEADS):
        att[x, block(z), h * HEAD : (h + 1) * HEAD] = merged[h]

    near = (0, 1, 7, 2, 6, 3, 5, 4)
    for e in (1, 3, 2):
        ax(0, e).start()
    for d in near[1:]:
        az(d).start()
    for d in near[1:]:
        az(d).wait_recv()
        for e in (1, 3, 2):
            ax(d, e).start()

    def project(source):
        rows = pl.ds(pl.multiple_of(source * CHUNK, CHUNK), CHUNK)
        t = dot(att[source], w_buf[...]).astype(jnp.bfloat16)
        terms[rows] = t
        for j in range(CHUNK // SHARE):
            owner = source * (CHUNK // SHARE) + j
            t_out[owner] = t[j * SHARE : (j + 1) * SHARE]

            @pl.when(owner != kvh)
            def _():
                tk((owner + NK - kvh) % NK).start()

    project(x)
    for e in (1, 3, 2):
        for d in near:
            ax(d, e).wait_recv()
        project((x + NX - e) % NX)

    partners = dot(pairs[...], terms[...]).astype(jnp.bfloat16)
    for i in range(NK):
        p_out[i] = partners[i * SHARE : (i + 1) * SHARE]
    for d in range(1, NK):
        pk(d).start()
    t_in[kvh] = t_out[kvh]
    p_in[kvh] = p_out[kvh]

    def total(ref):
        t = ref[0].astype(jnp.float32)
        for i in range(1, NK):
            t = t + ref[i].astype(jnp.float32)
        return t.astype(jnp.bfloat16)

    for d in range(1, NK):
        tk(d).wait_recv()
    total_ref[:, 0:OUT] = total(t_in)
    for d in range(1, NK):
        pk(d).wait_recv()
    total_ref[:, OUT:] = total(p_in)

    for n in range(NZ):
        for e in range(1, NX):
            if n not in (1, NZ - 1):
                fq(n, e).wait_send()
            px(n, e).wait_send()
            ax(n, e).wait_send()
    for e in range(1, NX):
        side(e, 0).wait_send()
        side(e, 1).wait_send()
    for k in range(1, NZ // 2 + 1):
        up(k).wait_send()
        if k < NZ // 2:
            down(k).wait_send()
    for d in range(1, NZ):
        pz(d).wait_send()
        az(d).wait_send()
    for d in range(1, NK):
        tk(d).wait_send()
        pk(d).wait_send()


def per_device(queries, keys, values, out_weight, positions, partner):
    bf, f32 = jnp.bfloat16, jnp.float32
    vmem = pl.BlockSpec(memory_space=pltpu.VMEM)
    any_ = pl.BlockSpec(memory_space=pl.ANY)
    dma = pltpu.SemaphoreType.DMA
    total = pl.pallas_call(
        kernel,
        out_shape=jax.ShapeDtypeStruct((SHARE, 2 * OUT), bf),
        in_specs=[vmem, any_, any_, any_, pl.BlockSpec(memory_space=pltpu.SMEM), vmem],
        out_specs=vmem,
        scratch_shapes=[
            pltpu.VMEM((LENGTH, HEAD), bf),
            pltpu.VMEM((LENGTH, HEAD), bf),
            pltpu.VMEM((COLS, OUT), bf),
            pltpu.VMEM((LENGTH, 2 * HEAD), bf),
            pltpu.VMEM((ROWS, LENGTH), f32),
            pltpu.VMEM((ROWS, LENGTH), f32),
            pltpu.VMEM((2, ROWS, 128), f32),
            pltpu.VMEM((NZ, SLAB, WIDE), bf),
            pltpu.VMEM((NZ + 3, SLAB, WIDE), bf),
            pltpu.VMEM((NZ + 3, NX - 1, TOK, WIDE), bf),
            pltpu.VMEM((NZ + 3, TOK, WIDE), bf),
            pltpu.VMEM((NZ, TOK, WIDE), bf),
            pltpu.VMEM((NX, CHUNK, COLS), bf),
            pltpu.VMEM((TOKENS, TOKENS), bf),
            pltpu.VMEM((TOKENS, OUT), bf),
            pltpu.VMEM((NK, SHARE, OUT), bf),
            pltpu.VMEM((NK, SHARE, OUT), bf),
            pltpu.VMEM((NK, SHARE, OUT), bf),
            pltpu.VMEM((NK, SHARE, OUT), bf),
            dma((3,)),
            dma((NZ, NX - 1)), dma((NZ, NX - 1)),
            dma((2, NX - 1)), dma((2, NX - 1)),
            dma((4,)), dma((4,)), dma((4,)), dma((4,)),
            dma((NZ, NX - 1)), dma((NZ, NX - 1)),
            dma((NZ - 1,)), dma((NZ - 1,)),
            dma((NZ - 1,)), dma((NZ - 1,)),
            dma((NZ, NX - 1)), dma((NZ, NX - 1)),
            dma((NK - 1,)), dma((NK - 1,)), dma((NK - 1,)), dma((NK - 1,)),
        ],
        compiler_params=pltpu.CompilerParams(
            collective_id=0, has_side_effects=True, vmem_limit_bytes=56 * 2**20),
    )(queries, keys, values, out_weight, positions, partner.reshape(1, TOKENS))
    mixed, other = total[:, 0:OUT], total[:, OUT:]
    return mixed, (mixed.astype(f32) - other.astype(f32)).astype(bf)


def solution(mesh):
    placed = (P("seq", "kvh"), P("seq", "kvh"), P("seq", "kvh"), P("kvh", "seq"), P("seq"), P())
    return jax.shard_map(
        per_device,
        mesh=mesh,
        in_specs=placed,
        out_specs=(P("kvh", "seq"), P("kvh", "seq")),
        check_vma=False,
    )
```
